32 devices in a mesh: lon: 8 (over y, x, core), lat: 4 (over z).
Axes of the slice: x: 2, y: 2, z: 4, core: 2. Of those that a mesh axis runs over, the one named last changes fastest.
Arguments:
- ocean_state: float32 [4, 8, 2048, 512], P(None, None, 'lon', 'lat'), may hold values from -6 to 6
- diffusivity: float32 [7, 2048, 512], P(None, 'lon', 'lat'), may hold values from 0.05 to 2
- land_mask: int32 [2048, 512], P('lon', 'lat'), may hold values from 0 to 1, as said below
- tile_plan: int32 [16, 4], P(None, 'lat'), may hold values from 0 to 15, as said below
Outputs:
- moved_state: float32 [4, 8, 2048, 512], P(None, None, 'lon', 'lat')
The draws below stay inside these ranges and needn't reach their ends.
Inputs may be any that keep to these rules, and one draw needn't show every extreme that they name: `land_mask`: tiles of 128 x 128 columns may be land throughout; others are ocean throughout or mixed. Each column of tile_plan is a permutation of 0 to 15; a tile whose columns are all land keeps its position; every tile lands within 3 tile positions of where it stands, counted around the longitude loop; in some row one tile moves 3 positions east and one 3 positions west.
All inputs are finite; a program needn't handle non-finite values.
Results may differ from the reference program's by a relative error of at most 0.00002.
Values sent between devices are 32-bit elements; how exact they have to be, the bound alone decides.
A program may use at most 128 MiB of HBM per device.

```python
import math
import jax
import jax.numpy as jnp

TILE = 128
LEVELS = 8
NX = 2048
NY = 512


def shared_layout(key):
    tile_total = NX // TILE
    row_total = NY // TILE
    tile_kind = jax.random.randint(jax.random.fold_in(key, 11), (tile_total, row_total), 0, 10)
    forced_row = jax.random.randint(jax.random.fold_in(key, 12), (), 0, row_total)
    second_row = (forced_row + 1) % row_total
    third_row = (forced_row + 2) % row_total
    row_index = jnp.arange(row_total)[None, :]
    forced_cell = (row_index == forced_row) | (row_index == second_row) | (row_index == third_row)
    tile_kind = jnp.where(forced_cell, 9, tile_kind)
    return (tile_kind, forced_row, second_row, third_row)


def draw_land_mask(key, part):
    tile_kind, forced_row, second_row, third_row = shared_layout(key)
    kind_cells = jnp.repeat(jnp.repeat(tile_kind, TILE, axis=0), TILE, axis=1)
    coastal = jax.random.randint(jax.random.fold_in(key, 14), (NX, NY), 0, 2)
    return jnp.where(kind_cells < 3, 0, jnp.where(kind_cells < 6, coastal, 1)).astype(jnp.int32)


def draw_tile_plan(key, part):
    tile_kind, forced_row, second_row, third_row = shared_layout(key)
    tile_total = NX // TILE
    row_total = NY // TILE
    group_total = tile_total // 4
    row_index = jnp.arange(row_total)
    phase = jax.random.randint(jax.random.fold_in(key, 15), (row_total,), 0, 4)
    phase = jnp.where(row_index == forced_row, 1, jnp.where(row_index == second_row, 3, jnp.where(row_index == third_row, 0, phase)))
    rotated_index = jnp.arange(tile_total)[:, None]
    real_of_rotated = (rotated_index + phase[None, :]) % tile_total
    kind_rotated = jnp.take_along_axis(tile_kind, real_of_rotated, axis=0)
    ocean = (kind_rotated >= 3).astype(jnp.int32).reshape(group_total, 4, row_total)
    local_index = jnp.arange(4)
    raw_keys = jax.random.randint(jax.random.fold_in(key, 16), (group_total, 4, row_total), 0, 1 << 20) * 4 + local_index[None, :, None]
    forced_here = (row_index[None, None, :] == forced_row) | (row_index[None, None, :] == second_row) | (row_index[None, None, :] == third_row)
    forced_here = jnp.broadcast_to(forced_here, (group_total, 4, row_total))
    sort_keys = jnp.where(forced_here, 3 - local_index[None, :, None], raw_keys)
    lower_mask = (local_index[:, None] < local_index[None, :]).astype(jnp.int32)
    ocean_rank = jnp.sum(ocean[:, :, None, :] * lower_mask[None, :, :, None], axis=1)
    smaller = (sort_keys[:, :, None, :] < sort_keys[:, None, :, :]).astype(jnp.int32)
    perm_rank = jnp.sum(ocean[:, :, None, :] * smaller, axis=1)
    match = (ocean[:, None, :, :] == 1) & (ocean_rank[:, None, :, :] == perm_rank[:, :, None, :])
    target_local = jnp.sum(match.astype(jnp.int32) * local_index[None, None, :, None], axis=2)
    target_local = jnp.where(ocean == 1, target_local, local_index[None, :, None])
    group_base = 4 * jnp.arange(group_total)[:, None, None]
    target_rotated = (group_base + target_local).reshape(tile_total, row_total)
    target_real = (target_rotated + phase[None, :]) % tile_total
    real_index = jnp.arange(tile_total)[:, None]
    rotated_of_real = (real_index - phase[None, :]) % tile_total
    return jnp.take_along_axis(target_real, rotated_of_real, axis=0).astype(jnp.int32)


def block_levels(rng, dims, cuts, low, largest):
    gain = 1.0
    for axis_at, parts in cuts:
        draws = jax.random.uniform(jax.random.fold_in(jax.random.fold_in(rng, 6), axis_at), (parts,), jnp.float32, low / len(cuts), largest / len(cuts))
        gain = gain * jnp.repeat(jnp.exp(draws), dims[axis_at] // parts).reshape((-1,) + (1,) * (len(dims) - 1 - axis_at))
    return gain


def normal_values(stream_key, dims, width, bound, split=(), kind=jnp.bfloat16):
    loudness = block_levels(stream_key, dims, split, -0.22, 0.18) if split else 1.0
    values = jax.random.normal(stream_key, dims, jnp.float32) * width * loudness
    return jnp.minimum(jnp.maximum(values, -bound), bound).astype(kind)


def setup_inputs(seed: int = 0) -> dict:
    seeds = jax.random.split(jax.random.key(seed), 5)
    ocean_state = normal_values(seeds[0], (4, LEVELS, NX, NY), 1.0, 6.0, ((2, 8), (3, 4)), jnp.float32)
    diffusivity = jnp.clip(jnp.exp(math.log(2.0) - 3.6888794 * jax.random.uniform(seeds[1], (LEVELS - 1, NX, NY), jnp.float32) ** block_levels(seeds[1], (LEVELS - 1, NX, NY), ((1, 8), (2, 4)), -0.2, 0.2)), 0.05, 2.0)
    land_mask = draw_land_mask(jax.random.fold_in(seeds[4], 71), 0)
    tile_plan = draw_tile_plan(jax.random.fold_in(seeds[4], 71), 0)
    return {"ocean_state": ocean_state, "diffusivity": diffusivity, "land_mask": land_mask, "tile_plan": tile_plan}


advect_coef = 0.1
diffuse_coef = 0.1
gradient_coef = 0.1
thermal_coef = 0.2
haline_coef = 0.15
weight_coef = 0.25
mixing_coef = 1.0


def tendency(padded, wet_mask):
    center = padded[:, :, 1:-1, 1:-1]
    east_cells = padded[:, :, 2:, 1:-1]
    west_cells = padded[:, :, :-2, 1:-1]
    north_cells = padded[:, :, 1:-1, 2:]
    south_cells = padded[:, :, 1:-1, :-2]
    density = haline_coef * padded[1] - thermal_coef * padded[0]
    pressure = weight_coef * jnp.cumsum(density, axis=0)
    zonal_gradient = pressure[:, 2:, 1:-1] - pressure[:, :-2, 1:-1]
    merid_gradient = pressure[:, 1:-1, 2:] - pressure[:, 1:-1, :-2]
    zonal_flow = center[2]
    meridional = center[3]
    advect = -advect_coef * (zonal_flow * (east_cells - west_cells) + meridional * (north_cells - south_cells))
    diffuse = diffuse_coef * (east_cells + west_cells + north_cells + south_cells - 4.0 * center)
    updated = center + advect + diffuse
    updated = updated.at[2].add(-gradient_coef * zonal_gradient)
    updated = updated.at[3].add(-gradient_coef * merid_gradient)
    return updated * wet_mask


def mix_columns(fields, diffusivity):
    levels = fields.shape[1]
    zero_band = jnp.zeros_like(diffusivity[0])
    lower_band = [zero_band] + [-mixing_coef * diffusivity[level_index - 1] for level_index in range(1, levels)]
    upper_band = [-mixing_coef * diffusivity[level_index] for level_index in range(levels - 1)] + [zero_band]
    sweep_upper = []
    sweep_rhs = []
    for level_index in range(levels):
        pivot_value = 1.0 - lower_band[level_index] - upper_band[level_index]
        rhs_level = fields[:, level_index]
        if level_index > 0:
            pivot_value = pivot_value - lower_band[level_index] * sweep_upper[level_index - 1]
            rhs_level = rhs_level - lower_band[level_index] * sweep_rhs[level_index - 1]
        sweep_upper.append(upper_band[level_index] / pivot_value)
        sweep_rhs.append(rhs_level / pivot_value)
    solution = [sweep_rhs[-1]]
    for level_index in range(levels - 2, -1, -1):
        solution.insert(0, sweep_rhs[level_index] - sweep_upper[level_index] * solution[0])
    return jnp.stack(solution, axis=1)


def fold_pad(fields):
    fold_signs = jnp.array([1.0, 1.0, -1.0, -1.0], jnp.float32)[:, None, None]
    lon_padded = jnp.concatenate([fields[:, :, -1:], fields, fields[:, :, :1]], axis=2)
    top_row = fields[:, :, ::-1, -1] * fold_signs
    corner_zero = jnp.zeros_like(top_row[:, :, :1])
    top_row = jnp.concatenate([corner_zero, top_row, corner_zero], axis=2)
    bottom_row = jnp.zeros_like(top_row)
    return jnp.concatenate([bottom_row[:, :, :, None], lon_padded, top_row[:, :, :, None]], axis=3)


def reference(ocean_state, diffusivity, land_mask, tile_plan):
    wet_mask = land_mask.astype(jnp.float32)
    fields = ocean_state * wet_mask
    padded = fold_pad(fields)
    stepped = tendency(padded, wet_mask)
    mixed_fields = mix_columns(stepped, diffusivity) * wet_mask
    tile_count = tile_plan.shape[0]
    row_count = tile_plan.shape[1]
    field_count = mixed_fields.shape[0]
    levels = mixed_fields.shape[1]
    total_x = mixed_fields.shape[2]
    tile_width = total_x // tile_count
    band_height = mixed_fields.shape[3] // row_count
    pieces = []
    for row_index in range(row_count):
        lat_band = mixed_fields[:, :, :, row_index * band_height:(row_index + 1) * band_height]
        lat_band = lat_band.reshape(field_count, levels, tile_count, tile_width, band_height)
        placed = jnp.zeros_like(lat_band).at[:, :, tile_plan[:, row_index]].set(lat_band)
        pieces.append(placed.reshape(field_count, levels, total_x, band_height))
    return jnp.concatenate(pieces, axis=3)
```

```python
import functools

import jax
import jax.numpy as jnp
from jax import lax
from jax.experimental import pallas as pl
from jax.experimental.pallas import tpu as pltpu
from jax.sharding import PartitionSpec as P

advect_coef = 0.1
diffuse_coef = 0.1
gradient_coef = 0.1
thermal_coef = 0.2
haline_coef = 0.15
weight_coef = 0.25

F32 = jnp.float32
MIB = 1 << 20
CHUNKS = 2


def edges_kernel(state_ref, mask_ref, lat_ref, lon_ref):
    levels, rows, lanes = state_ref.shape[1:]
    half = rows // 2
    field = pl.program_id(0)
    lane = lax.broadcasted_iota(jnp.int32, (8, lanes), 1)

    @pl.when(field == 0)
    def _():
        lat_ref[...] = jnp.zeros_like(lat_ref)

    def group(g, _):
        part = jnp.zeros((8, lanes), F32)
        for slot in range(2):
            at = pl.ds(pl.multiple_of(slot * half + g * 8, 8), 8)
            wet = mask_ref[at, :].astype(F32)
            for k in range(levels):
                x = state_ref[0, k, at, :] * wet
                place = 64 * slot + 2 * k
                part = jnp.where((lane >> 1) == (place >> 1), pltpu.roll(x, place + 1, 1), part)
        to = pl.ds(pl.multiple_of(g * 8, 8), 8)
        lat_ref[to, :] += pltpu.roll(part, field * (2 * levels), 1)
        return 0

    lax.fori_loop(0, half // 8, group, 0)
    for k in range(levels):
        lon_ref[0, k : k + 1, :] = state_ref[0, k, 0:1, :] * mask_ref[0:1, :].astype(F32)
        lon_ref[1, k : k + 1, :] = (
            state_ref[0, k, rows - 1 : rows, :] * mask_ref[rows - 1 : rows, :].astype(F32)
        )


def edges(state, mask):
    fields, levels, rows, lanes = state.shape
    return pl.pallas_call(
        edges_kernel,
        grid=(fields,),
        in_specs=[
            pl.BlockSpec((1, levels, rows, lanes), lambda f: (f, 0, 0, 0)),
            pl.BlockSpec((rows, lanes), lambda f: (0, 0)),
        ],
        out_specs=[
            pl.BlockSpec((rows // 2, lanes), lambda f: (0, 0)),
            pl.BlockSpec((2, levels, lanes), lambda f: (0, f, 0)),
        ],
        out_shape=[
            jax.ShapeDtypeStruct((rows // 2, lanes), F32),
            jax.ShapeDtypeStruct((2, fields * levels, lanes), F32),
        ],
        compiler_params=pltpu.CompilerParams(vmem_limit_bytes=24 * MIB),
    )(state, mask)


def step_kernel(
    state_ref, diff_ref, mask_ref, north_ref, south_ref, west_ref, east_ref, theirs_ref, mine_ref, padded
):
    fields, levels, rows, lanes = state_ref.shape
    quarter = rows // 4
    at_step = pl.program_id(0)
    core = lax.rem(lax.axis_index("lon"), 2)
    lane = lax.broadcasted_iota(jnp.int32, (8, lanes), 1)

    @pl.when(at_step == 0)
    def _():
        def fill(g, _):
            at = pl.ds(pl.multiple_of(g * 8, 8), 8)
            to = pl.ds(pl.multiple_of(g * 8 + 8, 8), 8)
            wet = mask_ref[at, :].astype(F32)
            for f in range(fields):
                for k in range(levels):
                    padded[f, k, to, :] = state_ref[f, k, at, :] * wet
            return 0

        lax.fori_loop(0, rows // 8, fill, 0)
        for f in range(fields):
            for k in range(levels):
                i = f * levels + k
                padded[f, k, 7:8, :] = west_ref[i : i + 1, :]
                padded[f, k, rows + 8 : rows + 9, :] = east_ref[i : i + 1, :]

    slot = lax.rem(at_step, 2)
    half = jnp.where(at_step < 2, 1 - core, core)
    is_last = lane == lanes - 1
    is_first = lane == 0

    def make(out_ref):
        def group(g, _):
            row = pl.multiple_of(half * quarter + g * 8, 8)
            base = pl.multiple_of(slot * (2 * quarter) + row, 8)
            north_pack = pltpu.roll(north_ref[pl.ds(row, 8), :], 64 * slot, 1)
            south_pack = pltpu.roll(south_ref[pl.ds(row, 8), :], 64 * slot, 1)
            wet = mask_ref[pl.ds(base, 8), :].astype(F32)
            zonal = meridional = None
            carry = None
            upper = []
            rhs = []
            for k in range(levels):
                center = [padded[f, k, pl.ds(base + 8, 8), :] for f in range(fields)]
                grad_x, grad_y, total = [], [], []
                for f in range(fields):
                    i = f * levels + k
                    e = padded[f, k, pl.ds(base + 9, 8), :]
                    w = padded[f, k, pl.ds(base + 7, 8), :]
                    n = jnp.where(
                        is_last,
                        pltpu.roll(north_pack, (lanes - 1 - (2 * i + 1)) % lanes, 1),
                        pltpu.roll(center[f], lanes - 1, 1),
                    )
                    s = jnp.where(
                        is_first,
                        pltpu.roll(south_pack, (lanes - 2 * i) % lanes, 1),
                        pltpu.roll(center[f], 1, 1),
                    )
                    grad_x.append(e - w)
                    grad_y.append(n - s)
                    total.append((e + w) + (n + s))
                dx = haline_coef * grad_x[1] - thermal_coef * grad_x[0]
                dy = haline_coef * grad_y[1] - thermal_coef * grad_y[0]
                zonal = dx if k == 0 else zonal + dx
                meridional = dy if k == 0 else meridional + dy
                u, v = center[2], center[3]
                lower_k = diff_ref[k - 1, pl.ds(base, 8), :] if k > 0 else None
                upper_k = diff_ref[k, pl.ds(base, 8), :] if k < levels - 1 else None
                pivot = 1.0
                if k > 0:
                    pivot = pivot + lower_k
                if k < levels - 1:
                    pivot = pivot + upper_k
                if k > 0:
                    pivot = pivot - lower_k * upper[k - 1]
                inverse = 1.0 / pivot
                upper.append(upper_k * inverse if k < levels - 1 else None)
                row_rhs = []
                for f in range(fields):
                    flow = u * grad_x[f] + v * grad_y[f]
                    value = (1.0 - 4.0 * diffuse_coef) * center[f] + (
                        diffuse_coef * total[f] - advect_coef * flow
                    )
                    if f == 2:
                        value = value - (gradient_coef * weight_coef) * zonal
                    if f == 3:
                        value = value - (gradient_coef * weight_coef) * meridional
                    if k > 0:
                        value = value + lower_k * rhs[k - 1][f]
                    row_rhs.append(value * inverse)
                rhs.append(row_rhs)
            to = pl.ds(pl.multiple_of(g * 8, 8), 8)
            for f in range(fields):
                x = rhs[levels - 1][f]
                out_ref[0, f, levels - 1, to, :] = x * wet
                for k in range(levels - 2, -1, -1):
                    x = rhs[k][f] + upper[k] * x
                    out_ref[0, f, k, to, :] = x * wet
            return 0

        lax.fori_loop(0, quarter // 8, group, 0)

    @pl.when(at_step < 2)
    def _():
        make(theirs_ref)

    @pl.when(at_step >= 2)
    def _():
        make(mine_ref)


def step(state, diffusivity, mask, north, south, west, east):
    fields, levels, rows, lanes = state.shape
    whole = lambda a: pl.BlockSpec(a.shape, lambda i, nd=a.ndim: (0,) * nd)
    block = (1, fields, levels, rows // 4, lanes)
    shape = jax.ShapeDtypeStruct((2, fields, levels, rows // 4, lanes), F32)
    return pl.pallas_call(
        step_kernel,
        grid=(4,),
        in_specs=[whole(a) for a in (state, diffusivity, mask, north, south, west, east)],
        out_specs=[
            pl.BlockSpec(block, lambda i: (jnp.minimum(i, 1), 0, 0, 0, 0)),
            pl.BlockSpec(block, lambda i: (jnp.maximum(i - 2, 0), 0, 0, 0, 0)),
        ],
        out_shape=[shape, shape],
        scratch_shapes=[pltpu.VMEM((fields, levels, rows + 16, lanes), F32)],
        compiler_params=pltpu.CompilerParams(vmem_limit_bytes=40 * MIB),
    )(state, diffusivity, mask, north, south, west, east)


def chip_of():
    return lax.axis_index("lon") // 2, lax.rem(lax.axis_index("lon"), 2)


def leaves(plan_ref, chips, chip, t, way):
    target = plan_ref[4 * chip + t] // 4
    return target == lax.rem(chip + way + chips, chips)


def pack_kernel(rounds, chips, plan_ref, mine, other, *rest):
    outs, sem = rest[:-1], rest[-1]
    chip, core = chip_of()
    fields = mine.shape[1]
    span = fields // CHUNKS
    at = 0
    jobs = []
    for way in (1, -1):
        for r in range(rounds):
            count = jnp.int32(0)
            chosen = jnp.int32(0)
            for t in range(4):
                hit = leaves(plan_ref, chips, chip, t, way)
                chosen = jnp.where(hit & (count == r), t, chosen)
                count = count + hit.astype(jnp.int32)
            jobs.append((way, r, chosen))
    for chunk in range(CHUNKS):
        for way, r, chosen in jobs:
            out = outs[chunk * 2 + (0 if way == 1 else 1)]
            own = chosen // 2 == core
            slot = lax.rem(chosen, 2)
            for is_own, source in ((True, mine), (False, other)):
                copy = pltpu.make_async_copy(
                    source.at[slot, pl.ds(chunk * span, span)], out.at[r], sem.at[at]
                )
                pl.when(own if is_own else jnp.logical_not(own))(copy.start)
            at += 1
    at = 0
    for chunk in range(CHUNKS):
        for way, r, chosen in jobs:
            out = outs[chunk * 2 + (0 if way == 1 else 1)]
            pltpu.make_async_copy(mine.at[0, pl.ds(chunk * span, span)], out.at[r], sem.at[at]).wait()
            at += 1


def place_kernel(rounds, chips, plan_ref, *rest):
    mine, theirs, other, other_theirs = rest[:4]
    arrived = rest[4:-2]
    out, sem = rest[-2:]
    chip, core = chip_of()
    fields, quarter = mine.shape[1], mine.shape[3]
    span = fields // CHUNKS
    tiles = 4 * chips
    waits = []
    for slot in range(2):
        target = 2 * lax.axis_index("lon") + slot
        source = jnp.int32(0)
        for shift in range(-3, 4):
            g = lax.rem(target + shift + tiles, tiles)
            source = jnp.where(plan_ref[g] == target, g, source)
        from_chip = source // 4
        t = lax.rem(source, 4)
        local = from_chip == chip
        own = t // 2 == core
        tslot = lax.rem(t, 2)
        for part in range(2):
            half = core if part == 0 else 1 - core
            row = pl.multiple_of(2 * quarter * slot + half * quarter, quarter)
            for chunk in range(CHUNKS):
                where_f = pl.ds(chunk * span, span)
                to = out.at[where_f, :, pl.ds(row, quarter), :]
                s = sem.at[(slot * 2 + part) * CHUNKS + chunk]
                held = mine if part == 0 else theirs
                held_other = other if part == 0 else other_theirs
                pl.when(local & own)(
                    pltpu.make_async_copy(held.at[tslot, where_f], to, s).start
                )
                pl.when(local & jnp.logical_not(own))(
                    pltpu.make_async_copy(held_other.at[tslot, where_f], to, s).start
                )
                for side, way in enumerate((1, -1)):
                    came = from_chip == lax.rem(chip - way + chips, chips)
                    rank = jnp.int32(0)
                    for q in range(3):
                        hit = leaves(plan_ref, chips, from_chip, q, way) & (q < t)
                        rank = rank + hit.astype(jnp.int32)
                    rank = jnp.minimum(rank, rounds - 1)
                    buffer = arrived[(part * CHUNKS + chunk) * 2 + side]
                    pl.when(came)(pltpu.make_async_copy(buffer.at[rank], to, s).start)
                waits.append((held.at[0, where_f], to, s))
    for a, b, s in waits:
        pltpu.make_async_copy(a, b, s).wait()


def exchange(rounds, plan, mine, theirs, other):
    devices = lax.axis_size("lon")
    chips = devices // 2
    fields, levels, quarter, lanes = mine.shape[1:]
    span = fields // CHUNKS
    swap = [(i, i ^ 1) for i in range(devices)]
    anywhere = pl.BlockSpec(memory_space=pl.ANY)
    scalars = pl.BlockSpec(memory_space=pltpu.SMEM)
    piece = jax.ShapeDtypeStruct((rounds, span, levels, quarter, lanes), F32)
    sends = pl.pallas_call(
        functools.partial(pack_kernel, rounds, chips),
        in_specs=[scalars, anywhere, anywhere],
        out_specs=[anywhere] * (2 * CHUNKS),
        out_shape=[piece] * (2 * CHUNKS),
        scratch_shapes=[pltpu.SemaphoreType.DMA((2 * CHUNKS * rounds,))],
    )(plan, mine, other)
    arrived = []
    for at, send in enumerate(sends):
        by = 2 if at % 2 == 0 else -2
        arrived.append(lax.ppermute(send, "lon", [(i, (i + by) % devices) for i in range(devices)]))
    other_theirs = lax.ppermute(mine, "lon", swap)
    swapped = [lax.ppermute(a, "lon", swap) for a in arrived]
    return pl.pallas_call(
        functools.partial(place_kernel, rounds, chips),
        in_specs=[scalars] + [anywhere] * (4 + 4 * CHUNKS),
        out_specs=anywhere,
        out_shape=jax.ShapeDtypeStruct((fields, levels, 4 * quarter, lanes), F32),
        scratch_shapes=[pltpu.SemaphoreType.DMA((4 * CHUNKS,))],
    )(plan, mine, theirs, other, other_theirs, *arrived, *swapped)


def most_rounds(plan, chips):
    target = (plan // 4).reshape(chips, 4)
    home = jnp.arange(chips, dtype=jnp.int32)[:, None]
    apart = jnp.mod(target - home, chips)
    east = jnp.max(jnp.sum((apart == 1).astype(jnp.int32), axis=1))
    west = jnp.max(jnp.sum((apart == chips - 1).astype(jnp.int32), axis=1))
    most = jnp.maximum(east, west)
    rows = lax.axis_size("lat")
    apart = 1
    while apart < rows:
        most = jnp.maximum(most, lax.ppermute(most, "lat", [(i, i ^ apart) for i in range(rows)]))
        apart *= 2
    return most


def local(state, diffusivity, mask, tile_plan):
    devices, bands = lax.axis_size("lon"), lax.axis_size("lat")
    plan = tile_plan.reshape(-1)
    most = most_rounds(plan, devices // 2)
    lat_pack, lon_pack = edges(state, mask)
    fold = lax.ppermute(
        lat_pack,
        ("lon", "lat"),
        [(i * bands + bands - 1, (devices - 1 - i) * bands + bands - 1) for i in range(devices)],
    )
    above = lax.ppermute(lat_pack, "lat", [(i + 1, i) for i in range(bands - 1)])
    south = lax.ppermute(lat_pack, "lat", [(i, i + 1) for i in range(bands - 1)])
    west = lax.ppermute(lon_pack[1], "lon", [(i, (i + 1) % devices) for i in range(devices)])
    east = lax.ppermute(lon_pack[0], "lon", [((i + 1) % devices, i) for i in range(devices)])
    lanes = state.shape[3]
    sign = jnp.where(jnp.arange(lanes) % 64 >= 32, -1.0, 1.0).astype(F32)
    mirror = jnp.roll(fold[::-1], 65, axis=1) * sign
    north = jnp.where(lax.axis_index("lat") == bands - 1, mirror, above)
    theirs, mine = step(state, diffusivity, mask, north, south, west, east)
    other = lax.ppermute(theirs, "lon", [(i, i ^ 1) for i in range(devices)])
    branches = [functools.partial(exchange, rounds) for rounds in (1, 2, 3)]
    return lax.switch(jnp.clip(most - 1, 0, 2), branches, plan, mine, theirs, other)


def solution(mesh):
    placed = (P(None, None, "lon", "lat"), P(None, "lon", "lat"), P("lon", "lat"), P(None, "lat"))
    return jax.shard_map(
        local, mesh=mesh, in_specs=placed, out_specs=P(None, None, "lon", "lat"), check_vma=False
    )
```

```python
import functools

import jax
import jax.numpy as jnp
from jax import lax
from jax.experimental import pallas as pl
from jax.experimental.pallas import tpu as pltpu
from jax.sharding import PartitionSpec as P

advect_coef = 0.1
diffuse_coef = 0.1
gradient_coef = 0.1
thermal_coef = 0.2
haline_coef = 0.15
weight_coef = 0.25

F32 = jnp.float32
MIB = 1 << 20
MESH = pl.DeviceIdType.MESH
CHUNKS = 2


def halo_kernel(
    plan_ref,
    state_ref,
    mask_ref,
    north_ref,
    south_ref,
    west_ref,
    east_ref,
    most_ref,
    lat_pack,
    lon_pack,
    north_in,
    south_in,
    west_in,
    east_in,
    count,
    counts_in,
    send_sem,
    recv_sem,
):
    levels, rows, lanes = state_ref.shape[1:]
    half = rows // 2
    field = pl.program_id(0)
    last_field = pl.num_programs(0) - 1
    lane = lax.broadcasted_iota(jnp.int32, (8, lanes), 1)
    devices, bands = lax.axis_size("lon"), lax.axis_size("lat")
    lon, lat = lax.axis_index("lon"), lax.axis_index("lat")
    top = lat == bands - 1
    to_east = {"lon": lax.rem(lon + 1, devices)}
    to_west = {"lon": lax.rem(lon + devices - 1, devices)}
    across = {"lon": devices - 1 - lon}
    others = [{"lat": lax.rem(lat + o, bands)} for o in range(1, bands)]
    barrier = pltpu.get_barrier_semaphore()

    @pl.when(field == 0)
    def _():
        for who in [to_east, to_west, across] + others:
            pl.semaphore_signal(barrier, inc=1, device_id=who, device_id_type=MESH)

        lat_pack[...] = jnp.zeros_like(lat_pack)

    unroll = 4

    def group(g, _):
        for sub in range(unroll):
            part = jnp.zeros((8, lanes), F32)
            for slot in range(2):
                at = pl.ds(pl.multiple_of(slot * half + (g * unroll + sub) * 8, 8), 8)
                wet = mask_ref[at, :].astype(F32)
                for k in range(levels):
                    x = state_ref[0, k, at, :] * wet
                    place = 64 * slot + 2 * k
                    part = jnp.where((lane >> 1) == (place >> 1), pltpu.roll(x, place + 1, 1), part)
            to = pl.ds(pl.multiple_of((g * unroll + sub) * 8, 8), 8)
            lat_pack[to, :] += pltpu.roll(part, field * (2 * levels), 1)
        return 0

    lax.fori_loop(0, half // (8 * unroll), group, 0)
    at_field = pl.ds(pl.multiple_of(field * levels, levels), levels)
    first = mask_ref[0:1, :].astype(F32)
    final = mask_ref[rows - 1 : rows, :].astype(F32)
    lon_pack[0, at_field, :] = jnp.concatenate([state_ref[0, k, 0:1, :] for k in range(levels)], 0) * first
    lon_pack[1, at_field, :] = (
        jnp.concatenate([state_ref[0, k, rows - 1 : rows, :] for k in range(levels)], 0) * final
    )

    @pl.when(field == last_field)
    def _():
        chips = devices // 2
        most = jnp.int32(1)
        for chip in range(chips):
            for way in (1, -1):
                number = jnp.int32(0)
                for t in range(4):
                    number = number + leaves(plan_ref, chips, chip, t, way).astype(jnp.int32)
                most = jnp.maximum(most, number)
        count[...] = jnp.full(count.shape, most, jnp.int32)
        pl.semaphore_wait(barrier, 3 + bands - 1)

        def remote(source, target, at, recv_at, who):
            return pltpu.make_async_remote_copy(
                src_ref=source,
                dst_ref=target,
                send_sem=send_sem.at[at],
                recv_sem=recv_sem.at[recv_at],
                device_id=who,
                device_id_type=MESH,
            )

        up = remote(lat_pack, south_in, 0, 0, {"lat": jnp.minimum(lat + 1, bands - 1)})
        down = remote(lat_pack, north_in, 1, 1, {"lat": jnp.maximum(lat - 1, 0)})
        fold = remote(lat_pack, north_in, 0, 1, across)
        east = remote(lon_pack.at[1], west_in, 2, 2, to_east)
        west = remote(lon_pack.at[0], east_in, 3, 3, to_west)
        tell = [remote(count, counts_in.at[o], 4 + o, 4 + o, who) for o, who in enumerate(others)]
        pl.when(top)(fold.start)
        pl.when(jnp.logical_not(top))(up.start)
        pl.when(lat > 0)(down.start)
        east.start()
        west.start()
        for t in tell:
            t.start()

        pl.when(lat > 0)(up.wait_recv)

        @pl.when(lat > 0)
        def _():
            south_ref[...] = south_in[...]

        @pl.when(lat == 0)
        def _():
            south_ref[...] = jnp.zeros_like(south_ref)

        east.wait_recv()
        west_ref[...] = west_in[...]
        west.wait_recv()
        east_ref[...] = east_in[...]
        down.wait_recv()

        @pl.when(top)
        def _():
            r = lax.broadcasted_iota(jnp.int32, (half, half), 0)
            c = lax.broadcasted_iota(jnp.int32, (half, half), 1)
            turn = jnp.where(r + c == half - 1, 1.0, 0.0).astype(F32)
            mirror = jnp.dot(
                turn, north_in[...], precision=lax.Precision.HIGHEST, preferred_element_type=F32
            )
            place = lax.broadcasted_iota(jnp.int32, (half, lanes), 1)
            mirror = pltpu.roll(mirror, 65, 1)
            north_ref[...] = jnp.where((place & 63) >= 32, -mirror, mirror)

        @pl.when(jnp.logical_not(top))
        def _():
            north_ref[...] = north_in[...]

        value = count[...]
        for o, t in enumerate(tell):
            t.wait_recv()
            value = jnp.maximum(value, counts_in[o])
        most_ref[...] = value
        up.wait_send()
        pl.when(lat > 0)(down.wait_send)
        east.wait_send()
        west.wait_send()
        for t in tell:
            t.wait_send()


def halos(plan, state, mask):
    fields, levels, rows, lanes = state.shape
    bands = lax.axis_size("lat")
    pack = (rows // 2, lanes)
    edge = (fields * levels, lanes)
    spec = lambda shape: pl.BlockSpec(shape, lambda f: (0, 0))
    return pl.pallas_call(
        halo_kernel,
        grid=(fields,),
        in_specs=[
            pl.BlockSpec(memory_space=pltpu.SMEM),
            pl.BlockSpec((1, levels, rows, lanes), lambda f: (f, 0, 0, 0)),
            spec((rows, lanes)),
        ],
        out_specs=[spec(pack), spec(pack), spec(edge), spec(edge), spec((8, lanes))],
        out_shape=[
            jax.ShapeDtypeStruct(pack, F32),
            jax.ShapeDtypeStruct(pack, F32),
            jax.ShapeDtypeStruct(edge, F32),
            jax.ShapeDtypeStruct(edge, F32),
            jax.ShapeDtypeStruct((8, lanes), jnp.int32),
        ],
        scratch_shapes=[
            pltpu.VMEM(pack, F32),
            pltpu.VMEM((2,) + edge, F32),
            pltpu.VMEM(pack, F32),
            pltpu.VMEM(pack, F32),
            pltpu.VMEM(edge, F32),
            pltpu.VMEM(edge, F32),
            pltpu.VMEM((8, lanes), jnp.int32),
            pltpu.VMEM((bands - 1, 8, lanes), jnp.int32),
            pltpu.SemaphoreType.DMA((4 + bands - 1,)),
            pltpu.SemaphoreType.DMA((4 + bands - 1,)),
        ],
        compiler_params=pltpu.CompilerParams(
            collective_id=0, has_side_effects=True, vmem_limit_bytes=24 * MIB
        ),
    )(plan, state, mask)


def step_kernel(
    state_ref, diff_ref, mask_ref, north_ref, south_ref, west_ref, east_ref, theirs_ref, mine_ref, padded
):
    fields, levels, rows, lanes = state_ref.shape
    quarter = rows // 4
    at_step = pl.program_id(0)
    core = lax.rem(lax.axis_index("lon"), 2)
    lane = lax.broadcasted_iota(jnp.int32, (8, lanes), 1)

    @pl.when(at_step == 0)
    def _():
        def fill(g, _):
            at = pl.ds(pl.multiple_of(g * 8, 8), 8)
            to = pl.ds(pl.multiple_of(g * 8 + 8, 8), 8)
            wet = mask_ref[at, :].astype(F32)
            for f in range(fields):
                for k in range(levels):
                    padded[f, k, to, :] = state_ref[f, k, at, :] * wet
            return 0

        lax.fori_loop(0, rows // 8, fill, 0)
        for f in range(fields):
            for k in range(levels):
                i = f * levels + k
                padded[f, k, 7:8, :] = west_ref[i : i + 1, :]
                padded[f, k, rows + 8 : rows + 9, :] = east_ref[i : i + 1, :]

    slot = lax.rem(at_step, 2)
    half = jnp.where(at_step < 2, 1 - core, core)
    is_last = lane == lanes - 1
    is_first = lane == 0

    def make(out_ref):
        def group(g, _):
            row = pl.multiple_of(half * quarter + g * 8, 8)
            base = pl.multiple_of(slot * (2 * quarter) + row, 8)
            north_pack = pltpu.roll(north_ref[pl.ds(row, 8), :], 64 * slot, 1)
            south_pack = pltpu.roll(south_ref[pl.ds(row, 8), :], 64 * slot, 1)
            wet = mask_ref[pl.ds(base, 8), :].astype(F32)
            zonal = meridional = None
            carry = None
            upper = []
            rhs = []
            for k in range(levels):
                center = [padded[f, k, pl.ds(base + 8, 8), :] for f in range(fields)]
                grad_x, grad_y, total = [], [], []
                for f in range(fields):
                    i = f * levels + k
                    e = padded[f, k, pl.ds(base + 9, 8), :]
                    w = padded[f, k, pl.ds(base + 7, 8), :]
                    n = jnp.where(
                        is_last,
                        pltpu.roll(north_pack, (lanes - 1 - (2 * i + 1)) % lanes, 1),
                        pltpu.roll(center[f], lanes - 1, 1),
                    )
                    s = jnp.where(
                        is_first,
                        pltpu.roll(south_pack, (lanes - 2 * i) % lanes, 1),
                        pltpu.roll(center[f], 1, 1),
                    )
                    grad_x.append(e - w)
                    grad_y.append(n - s)
                    total.append((e + w) + (n + s))
                dx = haline_coef * grad_x[1] - thermal_coef * grad_x[0]
                dy = haline_coef * grad_y[1] - thermal_coef * grad_y[0]
                zonal = dx if k == 0 else zonal + dx
                meridional = dy if k == 0 else meridional + dy
                u, v = center[2], center[3]
                lower_k = diff_ref[k - 1, pl.ds(base, 8), :] if k > 0 else None
                upper_k = diff_ref[k, pl.ds(base, 8), :] if k < levels - 1 else None
                pivot = 1.0
                if k > 0:
                    pivot = pivot + lower_k
                if k < levels - 1:
                    pivot = pivot + upper_k
                if k > 0:
                    pivot = pivot - lower_k * upper[k - 1]
                inverse = 1.0 / pivot
                upper.append(upper_k * inverse if k < levels - 1 else None)
                row_rhs = []
                for f in range(fields):
                    flow = u * grad_x[f] + v * grad_y[f]
                    value = (1.0 - 4.0 * diffuse_coef) * center[f] + (
                        diffuse_coef * total[f] - advect_coef * flow
                    )
                    if f == 2:
                        value = value - (gradient_coef * weight_coef) * zonal
                    if f == 3:
                        value = value - (gradient_coef * weight_coef) * meridional
                    if k > 0:
                        value = value + lower_k * rhs[k - 1][f]
                    row_rhs.append(value * inverse)
                rhs.append(row_rhs)
            to = pl.ds(pl.multiple_of(g * 8, 8), 8)
            for f in range(fields):
                x = rhs[levels - 1][f]
                out_ref[0, f, levels - 1, to, :] = x * wet
                for k in range(levels - 2, -1, -1):
                    x = rhs[k][f] + upper[k] * x
                    out_ref[0, f, k, to, :] = x * wet
            return 0

        lax.fori_loop(0, quarter // 8, group, 0)

    @pl.when(at_step < 2)
    def _():
        make(theirs_ref)

    @pl.when(at_step >= 2)
    def _():
        make(mine_ref)


def step(state, diffusivity, mask, north, south, west, east):
    fields, levels, rows, lanes = state.shape
    whole = lambda a: pl.BlockSpec(a.shape, lambda i, nd=a.ndim: (0,) * nd)
    block = (1, fields, levels, rows // 4, lanes)
    shape = jax.ShapeDtypeStruct((2, fields, levels, rows // 4, lanes), F32)
    return pl.pallas_call(
        step_kernel,
        grid=(4,),
        in_specs=[whole(a) for a in (state, diffusivity, mask, north, south, west, east)],
        out_specs=[
            pl.BlockSpec(block, lambda i: (jnp.minimum(i, 1), 0, 0, 0, 0)),
            pl.BlockSpec(block, lambda i: (jnp.maximum(i - 2, 0), 0, 0, 0, 0)),
        ],
        out_shape=[shape, shape],
        scratch_shapes=[pltpu.VMEM((fields, levels, rows + 16, lanes), F32)],
        compiler_params=pltpu.CompilerParams(vmem_limit_bytes=40 * MIB),
    )(state, diffusivity, mask, north, south, west, east)


def chip_of():
    return lax.axis_index("lon") // 2, lax.rem(lax.axis_index("lon"), 2)


def leaves(plan_ref, chips, chip, t, way):
    target = plan_ref[4 * chip + t] // 4
    return target == lax.rem(chip + way + chips, chips)


def pack_kernel(rounds, chips, plan_ref, mine, other, *rest):
    outs, held, sem, out_sem = rest[:-3], rest[-3], rest[-2], rest[-1]
    chip, core = chip_of()
    fields = mine.shape[1]
    span = fields // CHUNKS
    at = 0
    jobs = []
    for way in (1, -1):
        for r in range(rounds):
            count = jnp.int32(0)
            chosen = jnp.int32(0)
            for t in range(4):
                hit = leaves(plan_ref, chips, chip, t, way)
                chosen = jnp.where(hit & (count == r), t, chosen)
                count = count + hit.astype(jnp.int32)
            jobs.append((way, r, chosen))
    for chunk in range(CHUNKS):
        for way, r, chosen in jobs:
            out = outs[chunk * 2 + (0 if way == 1 else 1)]
            own = chosen // 2 == core
            slot = lax.rem(chosen, 2)
            for is_own, source in ((True, mine), (False, other)):
                copy = pltpu.make_async_copy(
                    source.at[slot, pl.ds(chunk * span, span)], held.at[at], sem.at[at]
                )
                pl.when(own if is_own else jnp.logical_not(own))(copy.start)
            at += 1
    at = 0
    writes = []
    for chunk in range(CHUNKS):
        for way, r, chosen in jobs:
            out = outs[chunk * 2 + (0 if way == 1 else 1)]
            pltpu.make_async_copy(mine.at[0, pl.ds(chunk * span, span)], held.at[at], sem.at[at]).wait()
            writes.append(pltpu.make_async_copy(held.at[at], out.at[r], out_sem.at[at]))
            writes[-1].start()
            at += 1
    for write in writes:
        write.wait()


def place_kernel(rounds, chips, plan_ref, *rest):
    mine, theirs, other, other_theirs = rest[:4]
    arrived = rest[4:-4]
    out, kept, sem, out_sem = rest[-4:]
    chip, core = chip_of()
    fields, quarter = mine.shape[1], mine.shape[3]
    span = fields // CHUNKS
    tiles = 4 * chips
    waits = []
    for slot in range(2):
        target = 2 * lax.axis_index("lon") + slot
        source = jnp.int32(0)
        for shift in range(-3, 4):
            g = lax.rem(target + shift + tiles, tiles)
            source = jnp.where(plan_ref[g] == target, g, source)
        from_chip = source // 4
        t = lax.rem(source, 4)
        local = from_chip == chip
        own = t // 2 == core
        tslot = lax.rem(t, 2)
        for part in range(2):
            half = core if part == 0 else 1 - core
            row = pl.multiple_of(2 * quarter * slot + half * quarter, quarter)
            for chunk in range(CHUNKS):
                where_f = pl.ds(chunk * span, span)
                job = (slot * 2 + part) * CHUNKS + chunk
                to = kept.at[job]
                s = sem.at[job]
                held = mine if part == 0 else theirs
                held_other = other if part == 0 else other_theirs
                pl.when(local & own)(
                    pltpu.make_async_copy(held.at[tslot, where_f], to, s).start
                )
                pl.when(local & jnp.logical_not(own))(
                    pltpu.make_async_copy(held_other.at[tslot, where_f], to, s).start
                )
                for side, way in enumerate((1, -1)):
                    came = from_chip == lax.rem(chip - way + chips, chips)
                    rank = jnp.int32(0)
                    for q in range(3):
                        hit = leaves(plan_ref, chips, from_chip, q, way) & (q < t)
                        rank = rank + hit.astype(jnp.int32)
                    rank = jnp.minimum(rank, rounds - 1)
                    buffer = arrived[(part * CHUNKS + chunk) * 2 + side]
                    pl.when(came)(pltpu.make_async_copy(buffer.at[rank], to, s).start)
                waits.append((held.at[0, where_f], to, s, out.at[where_f, :, pl.ds(row, quarter), :], out_sem.at[job]))
    writes = []
    for a, b, s, to, out_s in waits:
        pltpu.make_async_copy(a, b, s).wait()
        writes.append(pltpu.make_async_copy(b, to, out_s))
        writes[-1].start()
    for write in writes:
        write.wait()


def exchange(rounds, plan, mine, theirs, other):
    devices = lax.axis_size("lon")
    chips = devices // 2
    fields, levels, quarter, lanes = mine.shape[1:]
    span = fields // CHUNKS
    swap = [(i, i ^ 1) for i in range(devices)]
    anywhere = pl.BlockSpec(memory_space=pl.ANY)
    scalars = pl.BlockSpec(memory_space=pltpu.SMEM)
    piece = jax.ShapeDtypeStruct((rounds, span, levels, quarter, lanes), F32)
    sends = pl.pallas_call(
        functools.partial(pack_kernel, rounds, chips),
        in_specs=[scalars, anywhere, anywhere],
        out_specs=[anywhere] * (2 * CHUNKS),
        out_shape=[piece] * (2 * CHUNKS),
        scratch_shapes=[
            pltpu.VMEM((2 * CHUNKS * rounds, span, levels, quarter, lanes), F32),
            pltpu.SemaphoreType.DMA((2 * CHUNKS * rounds,)),
            pltpu.SemaphoreType.DMA((2 * CHUNKS * rounds,)),
        ],
        compiler_params=pltpu.CompilerParams(vmem_limit_bytes=24 * MIB),
    )(plan, mine, other)
    arrived = []
    for at, send in enumerate(sends):
        by = 2 if at % 2 == 0 else -2
        arrived.append(lax.ppermute(send, "lon", [(i, (i + by) % devices) for i in range(devices)]))
    other_theirs = lax.ppermute(mine, "lon", swap)
    swapped = [lax.ppermute(a, "lon", swap) for a in arrived]
    return pl.pallas_call(
        functools.partial(place_kernel, rounds, chips),
        in_specs=[scalars] + [anywhere] * (4 + 4 * CHUNKS),
        out_specs=anywhere,
        out_shape=jax.ShapeDtypeStruct((fields, levels, 4 * quarter, lanes), F32),
        scratch_shapes=[
            pltpu.VMEM((4 * CHUNKS, span, levels, quarter, lanes), F32),
            pltpu.SemaphoreType.DMA((4 * CHUNKS,)),
            pltpu.SemaphoreType.DMA((4 * CHUNKS,)),
        ],
        compiler_params=pltpu.CompilerParams(vmem_limit_bytes=24 * MIB),
    )(plan, mine, theirs, other, other_theirs, *arrived, *swapped)


def local(state, diffusivity, mask, tile_plan):
    devices = lax.axis_size("lon")
    plan = tile_plan.reshape(-1)
    north, south, west, east, most = halos(plan, state, mask)
    theirs, mine = step(state, diffusivity, mask, north, south, west, east)
    other = lax.ppermute(theirs, "lon", [(i, i ^ 1) for i in range(devices)])
    branches = [functools.partial(exchange, rounds) for rounds in (1, 2, 3)]
    return lax.switch(jnp.clip(most[0, 0] - 1, 0, 2), branches, plan, mine, theirs, other)


def solution(mesh):
    placed = (P(None, None, "lon", "lat"), P(None, "lon", "lat"), P("lon", "lat"), P(None, "lat"))
    return jax.shard_map(
        local, mesh=mesh, in_specs=placed, out_specs=P(None, None, "lon", "lat"), check_vma=False
    )
```

```python
import functools

import jax
import jax.numpy as jnp
from jax import lax
from jax.experimental import pallas as pl
from jax.experimental.pallas import tpu as pltpu
from jax.sharding import PartitionSpec as P

advect_coef = 0.1
diffuse_coef = 0.1
gradient_coef = 0.1
thermal_coef = 0.2
haline_coef = 0.15
weight_coef = 0.25

F32 = jnp.float32
MIB = 1 << 20
MESH = pl.DeviceIdType.MESH
CHUNKS = 2


def halo_kernel(
    plan_ref,
    state_ref,
    mask_ref,
    north_ref,
    south_ref,
    west_ref,
    east_ref,
    most_ref,
    lat_pack,
    lon_pack,
    north_in,
    south_in,
    west_in,
    east_in,
    count,
    counts_in,
    send_sem,
    recv_sem,
):
    levels, rows, lanes = state_ref.shape[1:]
    half = rows // 2
    field = pl.program_id(0)
    last_field = pl.num_programs(0) - 1
    lane = lax.broadcasted_iota(jnp.int32, (8, lanes), 1)
    devices, bands = lax.axis_size("lon"), lax.axis_size("lat")
    lon, lat = lax.axis_index("lon"), lax.axis_index("lat")
    top = lat == bands - 1
    to_east = {"lon": lax.rem(lon + 1, devices)}
    to_west = {"lon": lax.rem(lon + devices - 1, devices)}
    across = {"lon": devices - 1 - lon}
    others = [{"lat": lax.rem(lat + o, bands)} for o in range(1, bands)]
    barrier = pltpu.get_barrier_semaphore()

    @pl.when(field == 0)
    def _():
        for who in [to_east, to_west, across] + others:
            pl.semaphore_signal(barrier, inc=1, device_id=who, device_id_type=MESH)

        lat_pack[...] = jnp.zeros_like(lat_pack)

    unroll = 8

    def group(g, _):
        for sub in range(unroll):
            part = jnp.zeros((8, lanes), F32)
            for slot in range(2):
                at = pl.ds(pl.multiple_of(slot * half + (g * unroll + sub) * 8, 8), 8)
                wet = mask_ref[at, :].astype(F32)
                for k in range(levels):
                    x = state_ref[0, k, at, :] * wet
                    place = 64 * slot + 2 * k
                    part = jnp.where((lane >> 1) == (place >> 1), pltpu.roll(x, place + 1, 1), part)
            to = pl.ds(pl.multiple_of((g * unroll + sub) * 8, 8), 8)
            lat_pack[to, :] += pltpu.roll(part, field * (2 * levels), 1)
        return 0

    lax.fori_loop(0, half // (8 * unroll), group, 0)
    at_field = pl.ds(pl.multiple_of(field * levels, levels), levels)
    first = mask_ref[0:1, :].astype(F32)
    final = mask_ref[rows - 1 : rows, :].astype(F32)
    lon_pack[0, at_field, :] = jnp.concatenate([state_ref[0, k, 0:1, :] for k in range(levels)], 0) * first
    lon_pack[1, at_field, :] = (
        jnp.concatenate([state_ref[0, k, rows - 1 : rows, :] for k in range(levels)], 0) * final
    )

    @pl.when(field == last_field)
    def _():
        chips = devices // 2
        most = jnp.int32(1)
        for chip in range(chips):
            for way in (1, -1):
                number = jnp.int32(0)
                for t in range(4):
                    number = number + leaves(plan_ref, chips, chip, t, way).astype(jnp.int32)
                most = jnp.maximum(most, number)
        count[...] = jnp.full(count.shape, most, jnp.int32)
        pl.semaphore_wait(barrier, 3 + bands - 1)

        def remote(source, target, at, recv_at, who):
            return pltpu.make_async_remote_copy(
                src_ref=source,
                dst_ref=target,
                send_sem=send_sem.at[at],
                recv_sem=recv_sem.at[recv_at],
                device_id=who,
                device_id_type=MESH,
            )

        up = remote(lat_pack, south_in, 0, 0, {"lat": jnp.minimum(lat + 1, bands - 1)})
        down = remote(lat_pack, north_in, 1, 1, {"lat": jnp.maximum(lat - 1, 0)})
        fold = remote(lat_pack, north_in, 0, 1, across)
        east = remote(lon_pack.at[1], west_in, 2, 2, to_east)
        west = remote(lon_pack.at[0], east_in, 3, 3, to_west)
        tell = [remote(count, counts_in.at[o], 4 + o, 4 + o, who) for o, who in enumerate(others)]
        pl.when(top)(fold.start)
        pl.when(jnp.logical_not(top))(up.start)
        pl.when(lat > 0)(down.start)
        east.start()
        west.start()
        for t in tell:
            t.start()

        pl.when(lat > 0)(up.wait_recv)

        @pl.when(lat > 0)
        def _():
            south_ref[...] = south_in[...]

        @pl.when(lat == 0)
        def _():
            south_ref[...] = jnp.zeros_like(south_ref)

        east.wait_recv()
        west_ref[...] = west_in[...]
        west.wait_recv()
        east_ref[...] = east_in[...]
        down.wait_recv()

        @pl.when(top)
        def _():
            r = lax.broadcasted_iota(jnp.int32, (half, half), 0)
            c = lax.broadcasted_iota(jnp.int32, (half, half), 1)
            turn = jnp.where(r + c == half - 1, 1.0, 0.0).astype(F32)
            mirror = jnp.dot(
                turn, north_in[...], precision=lax.Precision.HIGHEST, preferred_element_type=F32
            )
            place = lax.broadcasted_iota(jnp.int32, (half, lanes), 1)
            mirror = pltpu.roll(mirror, 65, 1)
            north_ref[...] = jnp.where((place & 63) >= 32, -mirror, mirror)

        @pl.when(jnp.logical_not(top))
        def _():
            north_ref[...] = north_in[...]

        value = count[...]
        for o, t in enumerate(tell):
            t.wait_recv()
            value = jnp.maximum(value, counts_in[o])
        most_ref[...] = value
        up.wait_send()
        pl.when(lat > 0)(down.wait_send)
        east.wait_send()
        west.wait_send()
        for t in tell:
            t.wait_send()


def halos(plan, state, mask):
    fields, levels, rows, lanes = state.shape
    bands = lax.axis_size("lat")
    pack = (rows // 2, lanes)
    edge = (fields * levels, lanes)
    spec = lambda shape: pl.BlockSpec(shape, lambda f: (0, 0))
    return pl.pallas_call(
        halo_kernel,
        grid=(fields,),
        in_specs=[
            pl.BlockSpec(memory_space=pltpu.SMEM),
            pl.BlockSpec((1, levels, rows, lanes), lambda f: (f, 0, 0, 0)),
            spec((rows, lanes)),
        ],
        out_specs=[spec(pack), spec(pack), spec(edge), spec(edge), spec((8, lanes))],
        out_shape=[
            jax.ShapeDtypeStruct(pack, F32),
            jax.ShapeDtypeStruct(pack, F32),
            jax.ShapeDtypeStruct(edge, F32),
            jax.ShapeDtypeStruct(edge, F32),
            jax.ShapeDtypeStruct((8, lanes), jnp.int32),
        ],
        scratch_shapes=[
            pltpu.VMEM(pack, F32),
            pltpu.VMEM((2,) + edge, F32),
            pltpu.VMEM(pack, F32),
            pltpu.VMEM(pack, F32),
            pltpu.VMEM(edge, F32),
            pltpu.VMEM(edge, F32),
            pltpu.VMEM((8, lanes), jnp.int32),
            pltpu.VMEM((bands - 1, 8, lanes), jnp.int32),
            pltpu.SemaphoreType.DMA((4 + bands - 1,)),
            pltpu.SemaphoreType.DMA((4 + bands - 1,)),
        ],
        compiler_params=pltpu.CompilerParams(
            collective_id=0, has_side_effects=True, vmem_limit_bytes=24 * MIB
        ),
    )(plan, state, mask)


def leaves(plan_ref, chips, chip, t, way):
    target = plan_ref[4 * chip + t] // 4
    return target == lax.rem(chip + way + chips, chips)


def pick(index, values):
    chosen = values[0]
    for at, value in enumerate(values[1:], 1):
        chosen = jnp.where(index == at, value, chosen)
    return chosen


def move_kernel(
    rounds,
    plan_ref,
    state_ref,
    diff_ref,
    mask_ref,
    north_ref,
    south_ref,
    west_ref,
    east_ref,
    out_ref,
    padded,
    mine,
    theirs,
    other,
    other_theirs,
    leaving,
    arrived,
    swapped,
    result,
    load_sem,
    store_sem,
    half_send,
    half_recv,
    tile_send,
    tile_recv,
    swap_send,
    swap_recv,
):
    fields, levels, rows, lanes = state_ref.shape
    quarter = rows // 4
    span = fields // CHUNKS
    devices = lax.axis_size("lon")
    chips = devices // 2
    tiles = 4 * chips
    lon = lax.axis_index("lon")
    chip, core = lon // 2, lax.rem(lon, 2)
    twin = {"lon": lon + 1 - 2 * core}
    ahead = {"lon": lax.rem(lon + 2, devices)}
    behind = {"lon": lax.rem(lon + devices - 2, devices)}
    ways = ((1, ahead), (-1, behind))

    barrier = pltpu.get_barrier_semaphore()
    for who in (twin, ahead, behind):
        pl.semaphore_signal(barrier, inc=1, device_id=who, device_id_type=MESH)

    loads = [
        pltpu.make_async_copy(state_ref.at[f], padded.at[f, :, pl.ds(8, rows), :], load_sem.at[f])
        for f in range(fields)
    ]
    for load in loads:
        load.start()

    chosen = {}
    for side, (way, _) in enumerate(ways):
        hits = [leaves(plan_ref, chips, chip, t, way) for t in range(4)]
        for r in range(rounds):
            count, tile = jnp.int32(0), jnp.int32(0)
            for t in range(4):
                tile = jnp.where(hits[t] & (count == r), t, tile)
                count = count + hits[t].astype(jnp.int32)
            chosen[side, r] = jnp.where(tile // 2 == core, 0, 2) + lax.rem(tile, 2)
    origin = []
    for slot in range(2):
        target = 2 * lon + slot
        source = jnp.int32(0)
        for shift in range(-3, 4):
            g = lax.rem(target + shift + tiles, tiles)
            source = jnp.where(plan_ref[g] == target, g, source)
        from_chip, t = source // 4, lax.rem(source, 4)
        at = jnp.where(t // 2 == core, 0, 2) + lax.rem(t, 2)
        for side, (way, _) in enumerate(ways):
            came = from_chip == lax.rem(chip - way + chips, chips)
            rank = jnp.int32(0)
            for q in range(3):
                hit = leaves(plan_ref, chips, from_chip, q, way) & (q < t)
                rank = rank + hit.astype(jnp.int32)
            at = jnp.where(came, 4 + side * rounds + jnp.minimum(rank, rounds - 1), at)
        origin.append(at)

    for f in range(fields):
        loads[f].wait()

        def cover(g, _):
            for sub in range(2):
                at = pl.ds(pl.multiple_of(g * 16 + sub * 8, 8), 8)
                to = pl.ds(pl.multiple_of(g * 16 + sub * 8 + 8, 8), 8)
                wet = mask_ref[at, :].astype(F32)
                for k in range(levels):
                    padded[f, k, to, :] = padded[f, k, to, :] * wet
            return 0

        lax.fori_loop(0, rows // 16, cover, 0)
        for k in range(levels):
            i = f * levels + k
            padded[f, k, 7:8, :] = west_ref[i : i + 1, :]
            padded[f, k, rows + 8 : rows + 9, :] = east_ref[i : i + 1, :]

    lane = lax.broadcasted_iota(jnp.int32, (8, lanes), 1)
    is_last = lane == lanes - 1
    is_first = lane == 0

    def solve(chunk, half, to_ref):
        work = list(range(chunk * span, chunk * span + span))
        forced = any(f >= 2 for f in work)
        touched = sorted(set(work) | ({0, 1} if forced else set()))

        def group(step, _):
            slot, g = step // (quarter // 8), lax.rem(step, quarter // 8)
            row = pl.multiple_of(half * quarter + g * 8, 8)
            base = pl.multiple_of(slot * (2 * quarter) + row, 8)
            north_pack = pltpu.roll(north_ref[pl.ds(row, 8), :], 64 * slot, 1)
            south_pack = pltpu.roll(south_ref[pl.ds(row, 8), :], 64 * slot, 1)
            wet = mask_ref[pl.ds(base, 8), :].astype(F32)
            zonal = meridional = None
            upper = []
            rhs = []
            for k in range(levels):
                u = padded[2, k, pl.ds(base + 8, 8), :]
                v = padded[3, k, pl.ds(base + 8, 8), :]
                center, grad_x, grad_y, total = {}, {}, {}, {}
                for f in touched:
                    i = f * levels + k
                    center[f] = {2: u, 3: v}.get(f)
                    if f < 2:
                        center[f] = padded[f, k, pl.ds(base + 8, 8), :]
                    e = padded[f, k, pl.ds(base + 9, 8), :]
                    w = padded[f, k, pl.ds(base + 7, 8), :]
                    n = jnp.where(
                        is_last,
                        pltpu.roll(north_pack, (lanes - 1 - (2 * i + 1)) % lanes, 1),
                        pltpu.roll(center[f], lanes - 1, 1),
                    )
                    s = jnp.where(
                        is_first,
                        pltpu.roll(south_pack, (lanes - 2 * i) % lanes, 1),
                        pltpu.roll(center[f], 1, 1),
                    )
                    grad_x[f] = e - w
                    grad_y[f] = n - s
                    if f in work:
                        total[f] = (e + w) + (n + s)
                if forced:
                    dx = haline_coef * grad_x[1] - thermal_coef * grad_x[0]
                    dy = haline_coef * grad_y[1] - thermal_coef * grad_y[0]
                    zonal = dx if k == 0 else zonal + dx
                    meridional = dy if k == 0 else meridional + dy
                lower_k = diff_ref[k - 1, pl.ds(base, 8), :] if k > 0 else None
                upper_k = diff_ref[k, pl.ds(base, 8), :] if k < levels - 1 else None
                pivot = 1.0
                if k > 0:
                    pivot = pivot + lower_k
                if k < levels - 1:
                    pivot = pivot + upper_k
                if k > 0:
                    pivot = pivot - lower_k * upper[k - 1]
                inverse = 1.0 / pivot
                upper.append(upper_k * inverse if k < levels - 1 else None)
                row_rhs = []
                for at, f in enumerate(work):
                    flow = u * grad_x[f] + v * grad_y[f]
                    value = (1.0 - 4.0 * diffuse_coef) * center[f] + (
                        diffuse_coef * total[f] - advect_coef * flow
                    )
                    if f == 2:
                        value = value - (gradient_coef * weight_coef) * zonal
                    if f == 3:
                        value = value - (gradient_coef * weight_coef) * meridional
                    if k > 0:
                        value = value + lower_k * rhs[k - 1][at]
                    row_rhs.append(value * inverse)
                rhs.append(row_rhs)
            to = pl.ds(pl.multiple_of(g * 8, 8), 8)
            for at, f in enumerate(work):
                x = rhs[levels - 1][at]
                to_ref[chunk, slot, at, levels - 1, to, :] = x * wet
                for k in range(levels - 2, -1, -1):
                    x = rhs[k][at] + upper[k] * x
                    to_ref[chunk, slot, at, k, to, :] = x * wet
            return 0

        lax.fori_loop(0, 2 * (quarter // 8), group, 0)

    def remote(source, target, send, recv, who):
        return pltpu.make_async_remote_copy(
            src_ref=source,
            dst_ref=target,
            send_sem=send,
            recv_sem=recv,
            device_id=who,
            device_id_type=MESH,
        )

    pl.semaphore_wait(barrier, 3)
    halves = []
    sent = {}
    for chunk in range(CHUNKS):
        solve(chunk, 1 - core, theirs)
        first = remote(
            theirs.at[chunk], other.at[chunk], half_send.at[chunk, 0], half_recv.at[chunk, 0], twin
        )
        first.start()
        solve(chunk, core, mine)
        second = remote(
            mine.at[chunk], other_theirs.at[chunk], half_send.at[chunk, 1], half_recv.at[chunk, 1], twin
        )
        halves += [first, second]
        first.wait_recv()
        for at in range(span):
            f = chunk * span + at

            def pack(k, _):
                held = [ref[chunk, slot, at, k] for ref in (mine, other) for slot in range(2)]
                for (side, r), index in chosen.items():
                    leaving[f, side, r, k] = pick(index, held)
                return 0

            lax.fori_loop(0, levels, pack, 0)
            for r in range(rounds):
                for side, (_, who) in enumerate(ways):
                    sent[f, side, r] = remote(
                        leaving.at[f, side, r],
                        arrived.at[f, side, r],
                        tile_send.at[f, side, r],
                        tile_recv.at[f, side, r],
                        who,
                    )
                    sent[f, side, r].start()
        second.start()

    keys = [(side, r) for side in range(2) for r in range(rounds)]
    passed = {}
    stores = []
    for chunk in range(CHUNKS):
        halves[2 * chunk + 1].wait_recv()

    def place(f):
        chunk, at = f // span, f % span
        for key in keys:
            passed[(f,) + key].wait_recv()

        def level(k, _):
            for part in range(2):
                held, far, came = (
                    (mine, other, arrived) if part == 0 else (theirs, other_theirs, swapped)
                )
                values = [ref[chunk, slot, at, k] for ref in (held, far) for slot in range(2)]
                values += [came[f, side, r, k] for side, r in keys]
                half = core if part == 0 else 1 - core
                for slot in range(2):
                    row = pl.multiple_of(2 * quarter * slot + half * quarter, quarter)
                    result[f, k, pl.ds(row, quarter), :] = pick(origin[slot], values)
            return 0

        lax.fori_loop(0, levels, level, 0)
        store = pltpu.make_async_copy(result.at[f], out_ref.at[f], store_sem.at[f])
        store.start()
        stores.append(store)

    for f in range(fields):
        for side, r in keys:
            sent[f, side, r].wait_recv()
            passed[f, side, r] = remote(
                arrived.at[f, side, r],
                swapped.at[f, side, r],
                swap_send.at[f, side, r],
                swap_recv.at[f, side, r],
                twin,
            )
            passed[f, side, r].start()
        if f > 0:
            place(f - 1)
    place(fields - 1)
    for copy in halves + list(sent.values()) + list(passed.values()):
        copy.wait_send()
    for store in stores:
        store.wait()


def move(rounds, plan, state, diffusivity, mask, north, south, west, east):
    fields, levels, rows, lanes = state.shape
    quarter = rows // 4
    span = fields // CHUNKS
    anywhere = pl.BlockSpec(memory_space=pl.ANY)
    near = pl.BlockSpec(memory_space=pltpu.VMEM)
    halves = pltpu.VMEM((CHUNKS, 2, span, levels, quarter, lanes), F32)
    pieces = pltpu.VMEM((fields, 2, rounds, levels, quarter, lanes), F32)
    dma = pltpu.SemaphoreType.DMA
    return pl.pallas_call(
        functools.partial(move_kernel, rounds),
        in_specs=[pl.BlockSpec(memory_space=pltpu.SMEM), anywhere] + [near] * 6,
        out_specs=anywhere,
        out_shape=jax.ShapeDtypeStruct(state.shape, F32),
        scratch_shapes=[
            pltpu.VMEM((fields, levels, rows + 16, lanes), F32),
            halves,
            halves,
            halves,
            halves,
            pieces,
            pieces,
            pieces,
            pltpu.VMEM(state.shape, F32),
            dma((fields,)),
            dma((fields,)),
            dma((CHUNKS, 2)),
            dma((CHUNKS, 2)),
            dma((fields, 2, rounds)),
            dma((fields, 2, rounds)),
            dma((fields, 2, rounds)),
            dma((fields, 2, rounds)),
        ],
        compiler_params=pltpu.CompilerParams(
            collective_id=rounds, has_side_effects=True, vmem_limit_bytes=(26 + 6 * rounds) * MIB
        ),
    )(plan, state, diffusivity, mask, north, south, west, east)


def local(state, diffusivity, mask, tile_plan):
    plan = tile_plan.reshape(-1)
    north, south, west, east, most = halos(plan, state, mask)
    branches = [functools.partial(move, rounds) for rounds in (1, 2, 3)]
    which = jnp.clip(most[0, 0] - 1, 0, 2)
    return lax.switch(which, branches, plan, state, diffusivity, mask, north, south, west, east)


def solution(mesh):
    placed = (P(None, None, "lon", "lat"), P(None, "lon", "lat"), P("lon", "lat"), P(None, "lat"))
    return jax.shard_map(
        local, mesh=mesh, in_specs=placed, out_specs=P(None, None, "lon", "lat"), check_vma=False
    )
```

```python
import functools

import jax
import jax.numpy as jnp
from jax import lax
from jax.experimental import pallas as pl
from jax.experimental.pallas import tpu as pltpu
from jax.sharding import PartitionSpec as P

advect_coef = 0.1
diffuse_coef = 0.1
gradient_coef = 0.1
thermal_coef = 0.2
haline_coef = 0.15
weight_coef = 0.25

F32 = jnp.float32
MIB = 1 << 20
MESH = pl.DeviceIdType.MESH
CHUNKS = 4


def halo_kernel(
    plan_ref,
    state_ref,
    mask_ref,
    north_ref,
    south_ref,
    west_ref,
    east_ref,
    most_ref,
    lat_pack,
    lon_pack,
    north_in,
    south_in,
    west_in,
    east_in,
    count,
    counts_in,
    send_sem,
    recv_sem,
):
    levels, rows, lanes = state_ref.shape[1:]
    half = rows // 2
    field = pl.program_id(0)
    last_field = pl.num_programs(0) - 1
    lane = lax.broadcasted_iota(jnp.int32, (8, lanes), 1)
    devices, bands = lax.axis_size("lon"), lax.axis_size("lat")
    lon, lat = lax.axis_index("lon"), lax.axis_index("lat")
    top = lat == bands - 1
    to_east = {"lon": lax.rem(lon + 1, devices)}
    to_west = {"lon": lax.rem(lon + devices - 1, devices)}
    across = {"lon": devices - 1 - lon}
    others = [{"lat": lax.rem(lat + o, bands)} for o in range(1, bands)]
    barrier = pltpu.get_barrier_semaphore()

    @pl.when(field == 0)
    def _():
        for who in [to_east, to_west, across] + others:
            pl.semaphore_signal(barrier, inc=1, device_id=who, device_id_type=MESH)

        lat_pack[...] = jnp.zeros_like(lat_pack)

    unroll = half // 8

    def group(g, _):
        for sub in range(unroll):
            part = jnp.zeros((8, lanes), F32)
            for slot in range(2):
                at = pl.ds(pl.multiple_of(slot * half + (g * unroll + sub) * 8, 8), 8)
                wet = mask_ref[at, :].astype(F32)
                for k in range(levels):
                    x = state_ref[0, k, at, :] * wet
                    place = 64 * slot + 2 * k
                    part = jnp.where((lane >> 1) == (place >> 1), pltpu.roll(x, place + 1, 1), part)
            to = pl.ds(pl.multiple_of((g * unroll + sub) * 8, 8), 8)
            lat_pack[to, :] += pltpu.roll(part, field * (2 * levels), 1)
        return 0

    lax.fori_loop(0, half // (8 * unroll), group, 0)
    at_field = pl.ds(pl.multiple_of(field * levels, levels), levels)
    first = mask_ref[0:1, :].astype(F32)
    final = mask_ref[rows - 1 : rows, :].astype(F32)
    lon_pack[0, at_field, :] = jnp.concatenate([state_ref[0, k, 0:1, :] for k in range(levels)], 0) * first
    lon_pack[1, at_field, :] = (
        jnp.concatenate([state_ref[0, k, rows - 1 : rows, :] for k in range(levels)], 0) * final
    )

    @pl.when(field == last_field)
    def _():
        chips = devices // 2
        most = jnp.int32(1)
        for chip in range(chips):
            for way in (1, -1):
                number = jnp.int32(0)
                for t in range(4):
                    number = number + leaves(plan_ref, chips, chip, t, way).astype(jnp.int32)
                most = jnp.maximum(most, number)
        count[...] = jnp.full(count.shape, most, jnp.int32)
        pl.semaphore_wait(barrier, 3 + bands - 1)

        def remote(source, target, at, recv_at, who):
            return pltpu.make_async_remote_copy(
                src_ref=source,
                dst_ref=target,
                send_sem=send_sem.at[at],
                recv_sem=recv_sem.at[recv_at],
                device_id=who,
                device_id_type=MESH,
            )

        up = remote(lat_pack, south_in, 0, 0, {"lat": jnp.minimum(lat + 1, bands - 1)})
        down = remote(lat_pack, north_in, 1, 1, {"lat": jnp.maximum(lat - 1, 0)})
        fold = remote(lat_pack, north_in, 0, 1, across)
        east = remote(lon_pack.at[1], west_in, 2, 2, to_east)
        west = remote(lon_pack.at[0], east_in, 3, 3, to_west)
        tell = [remote(count, counts_in.at[o], 4 + o, 4 + o, who) for o, who in enumerate(others)]
        pl.when(top)(fold.start)
        pl.when(jnp.logical_not(top))(up.start)
        pl.when(lat > 0)(down.start)
        east.start()
        west.start()
        for t in tell:
            t.start()

        pl.when(lat > 0)(up.wait_recv)

        @pl.when(lat > 0)
        def _():
            south_ref[...] = south_in[...]

        @pl.when(lat == 0)
        def _():
            south_ref[...] = jnp.zeros_like(south_ref)

        east.wait_recv()
        west_ref[...] = west_in[...]
        west.wait_recv()
        east_ref[...] = east_in[...]
        down.wait_recv()

        @pl.when(top)
        def _():
            r = lax.broadcasted_iota(jnp.int32, (half, half), 0)
            c = lax.broadcasted_iota(jnp.int32, (half, half), 1)
            turn = jnp.where(r + c == half - 1, 1.0, 0.0).astype(F32)
            mirror = jnp.dot(
                turn, north_in[...], precision=lax.Precision.HIGHEST, preferred_element_type=F32
            )
            place = lax.broadcasted_iota(jnp.int32, (half, lanes), 1)
            mirror = pltpu.roll(mirror, 65, 1)
            north_ref[...] = jnp.where((place & 63) >= 32, -mirror, mirror)

        @pl.when(jnp.logical_not(top))
        def _():
            north_ref[...] = north_in[...]

        value = count[...]
        for o, t in enumerate(tell):
            t.wait_recv()
            value = jnp.maximum(value, counts_in[o])
        most_ref[0] = jnp.max(value) - 1
        up.wait_send()
        pl.when(lat > 0)(down.wait_send)
        east.wait_send()
        west.wait_send()
        for t in tell:
            t.wait_send()


def halos(plan, state, mask):
    fields, levels, rows, lanes = state.shape
    bands = lax.axis_size("lat")
    pack = (rows // 2, lanes)
    edge = (fields * levels, lanes)
    spec = lambda shape: pl.BlockSpec(shape, lambda f: (0, 0))
    return pl.pallas_call(
        halo_kernel,
        grid=(fields,),
        in_specs=[
            pl.BlockSpec(memory_space=pltpu.SMEM),
            pl.BlockSpec((1, levels, rows, lanes), lambda f: (f, 0, 0, 0)),
            spec((rows, lanes)),
        ],
        out_specs=[spec(pack), spec(pack), spec(edge), spec(edge), pl.BlockSpec(memory_space=pltpu.SMEM)],
        out_shape=[
            jax.ShapeDtypeStruct(pack, F32),
            jax.ShapeDtypeStruct(pack, F32),
            jax.ShapeDtypeStruct(edge, F32),
            jax.ShapeDtypeStruct(edge, F32),
            jax.ShapeDtypeStruct((1,), jnp.int32),
        ],
        scratch_shapes=[
            pltpu.VMEM(pack, F32),
            pltpu.VMEM((2,) + edge, F32),
            pltpu.VMEM(pack, F32),
            pltpu.VMEM(pack, F32),
            pltpu.VMEM(edge, F32),
            pltpu.VMEM(edge, F32),
            pltpu.VMEM((8, lanes), jnp.int32),
            pltpu.VMEM((bands - 1, 8, lanes), jnp.int32),
            pltpu.SemaphoreType.DMA((4 + bands - 1,)),
            pltpu.SemaphoreType.DMA((4 + bands - 1,)),
        ],
        compiler_params=pltpu.CompilerParams(
            collective_id=0, has_side_effects=True, vmem_limit_bytes=24 * MIB
        ),
    )(plan, state, mask)


def leaves(plan_ref, chips, chip, t, way):
    target = plan_ref[4 * chip + t] // 4
    return target == lax.rem(chip + way + chips, chips)


def pick(index, values):
    chosen = values[0]
    for at, value in enumerate(values[1:], 1):
        chosen = jnp.where(index == at, value, chosen)
    return chosen


def move_kernel(
    rounds,
    plan_ref,
    state_ref,
    diff_ref,
    mask_ref,
    north_ref,
    south_ref,
    west_ref,
    east_ref,
    out_ref,
    padded,
    mine,
    theirs,
    other,
    other_theirs,
    leaving,
    arrived,
    swapped,
    result,
    load_sem,
    store_sem,
    half_send,
    half_recv,
    tile_send,
    tile_recv,
    swap_send,
    swap_recv,
):
    fields, levels, rows, lanes = state_ref.shape
    quarter = rows // 4
    span = fields // CHUNKS
    devices = lax.axis_size("lon")
    chips = devices // 2
    tiles = 4 * chips
    lon = lax.axis_index("lon")
    chip, core = lon // 2, lax.rem(lon, 2)
    twin = {"lon": lon + 1 - 2 * core}
    ahead = {"lon": lax.rem(lon + 2, devices)}
    behind = {"lon": lax.rem(lon + devices - 2, devices)}
    ways = ((1, ahead), (-1, behind))

    barrier = pltpu.get_barrier_semaphore()
    for who in (twin, ahead, behind):
        pl.semaphore_signal(barrier, inc=1, device_id=who, device_id_type=MESH)

    loads = [
        pltpu.make_async_copy(state_ref.at[f], padded.at[f, :, pl.ds(8, rows), :], load_sem.at[f])
        for f in range(fields)
    ]
    for f in (0, 2, 3, 1):
        loads[f].start()

    chosen = {}
    for side, (way, _) in enumerate(ways):
        hits = [leaves(plan_ref, chips, chip, t, way) for t in range(4)]
        for r in range(rounds):
            count, tile = jnp.int32(0), jnp.int32(0)
            for t in range(4):
                tile = jnp.where(hits[t] & (count == r), t, tile)
                count = count + hits[t].astype(jnp.int32)
            chosen[side, r] = jnp.where(tile // 2 == core, 0, 2) + lax.rem(tile, 2)
    origin = []
    for slot in range(2):
        target = 2 * lon + slot
        source = jnp.int32(0)
        for shift in range(-3, 4):
            g = lax.rem(target + shift + tiles, tiles)
            source = jnp.where(plan_ref[g] == target, g, source)
        from_chip, t = source // 4, lax.rem(source, 4)
        at = jnp.where(t // 2 == core, 0, 2) + lax.rem(t, 2)
        for side, (way, _) in enumerate(ways):
            came = from_chip == lax.rem(chip - way + chips, chips)
            rank = jnp.int32(0)
            for q in range(3):
                hit = leaves(plan_ref, chips, from_chip, q, way) & (q < t)
                rank = rank + hit.astype(jnp.int32)
            at = jnp.where(came, 4 + side * rounds + jnp.minimum(rank, rounds - 1), at)
        origin.append(at)

    def cover_field(f):
        def cover(g, _):
            for sub in range(2):
                at = pl.ds(pl.multiple_of(g * 16 + sub * 8, 8), 8)
                to = pl.ds(pl.multiple_of(g * 16 + sub * 8 + 8, 8), 8)
                wet = mask_ref[at, :].astype(F32)
                for k in range(levels):
                    padded[f, k, to, :] = padded[f, k, to, :] * wet
            return 0

        lax.fori_loop(0, rows // 16, cover, 0)
        for k in range(levels):
            i = f * levels + k
            padded[f, k, 7:8, :] = west_ref[i : i + 1, :]
            padded[f, k, rows + 8 : rows + 9, :] = east_ref[i : i + 1, :]

    lane = lax.broadcasted_iota(jnp.int32, (8, lanes), 1)
    is_last = lane == lanes - 1
    is_first = lane == 0

    def solve(chunk, half, to_ref):
        work = list(range(chunk * span, chunk * span + span))
        forced = any(f >= 2 for f in work)
        touched = sorted(set(work) | ({0, 1} if forced else set()))

        def group(step, _):
            slot, g = step // (quarter // 8), lax.rem(step, quarter // 8)
            row = pl.multiple_of(half * quarter + g * 8, 8)
            base = pl.multiple_of(slot * (2 * quarter) + row, 8)
            north_pack = pltpu.roll(north_ref[pl.ds(row, 8), :], 64 * slot, 1)
            south_pack = pltpu.roll(south_ref[pl.ds(row, 8), :], 64 * slot, 1)
            wet = mask_ref[pl.ds(base, 8), :].astype(F32)
            zonal = meridional = None
            upper = []
            rhs = []
            for k in range(levels):
                u = padded[2, k, pl.ds(base + 8, 8), :]
                v = padded[3, k, pl.ds(base + 8, 8), :]
                center, grad_x, grad_y, total = {}, {}, {}, {}
                for f in touched:
                    i = f * levels + k
                    center[f] = {2: u, 3: v}.get(f)
                    if f < 2:
                        center[f] = padded[f, k, pl.ds(base + 8, 8), :]
                    e = padded[f, k, pl.ds(base + 9, 8), :]
                    w = padded[f, k, pl.ds(base + 7, 8), :]
                    n = jnp.where(
                        is_last,
                        pltpu.roll(north_pack, (lanes - 1 - (2 * i + 1)) % lanes, 1),
                        pltpu.roll(center[f], lanes - 1, 1),
                    )
                    s = jnp.where(
                        is_first,
                        pltpu.roll(south_pack, (lanes - 2 * i) % lanes, 1),
                        pltpu.roll(center[f], 1, 1),
                    )
                    grad_x[f] = e - w
                    grad_y[f] = n - s
                    if f in work:
                        total[f] = (e + w) + (n + s)
                if forced:
                    dx = haline_coef * grad_x[1] - thermal_coef * grad_x[0]
                    dy = haline_coef * grad_y[1] - thermal_coef * grad_y[0]
                    zonal = dx if k == 0 else zonal + dx
                    meridional = dy if k == 0 else meridional + dy
                lower_k = diff_ref[k - 1, pl.ds(base, 8), :] if k > 0 else None
                upper_k = diff_ref[k, pl.ds(base, 8), :] if k < levels - 1 else None
                pivot = 1.0
                if k > 0:
                    pivot = pivot + lower_k
                if k < levels - 1:
                    pivot = pivot + upper_k
                if k > 0:
                    pivot = pivot - lower_k * upper[k - 1]
                inverse = 1.0 / pivot
                upper.append(upper_k * inverse if k < levels - 1 else None)
                row_rhs = []
                for at, f in enumerate(work):
                    flow = u * grad_x[f] + v * grad_y[f]
                    value = (1.0 - 4.0 * diffuse_coef) * center[f] + (
                        diffuse_coef * total[f] - advect_coef * flow
                    )
                    if f == 2:
                        value = value - (gradient_coef * weight_coef) * zonal
                    if f == 3:
                        value = value - (gradient_coef * weight_coef) * meridional
                    if k > 0:
                        value = value + lower_k * rhs[k - 1][at]
                    row_rhs.append(value * inverse)
                rhs.append(row_rhs)
            to = pl.ds(pl.multiple_of(g * 8, 8), 8)
            for at, f in enumerate(work):
                x = rhs[levels - 1][at]
                to_ref[chunk, slot, at, levels - 1, to, :] = x * wet
                for k in range(levels - 2, -1, -1):
                    x = rhs[k][at] + upper[k] * x
                    to_ref[chunk, slot, at, k, to, :] = x * wet
            return 0

        lax.fori_loop(0, 2 * (quarter // 8), group, 0)

    def remote(source, target, send, recv, who):
        return pltpu.make_async_remote_copy(
            src_ref=source,
            dst_ref=target,
            send_sem=send,
            recv_sem=recv,
            device_id=who,
            device_id_type=MESH,
        )

    halves = []
    sent = {}
    for chunk in range(CHUNKS):
        for f in (0, 2, 3) if chunk == 0 else (1,) if chunk == 1 else ():
            loads[f].wait()
        for f in range(chunk * span, chunk * span + span):
            cover_field(f)
        solve(chunk, 1 - core, theirs)
        if chunk == 0:
            pl.semaphore_wait(barrier, 3)
        first = remote(
            theirs.at[chunk], other.at[chunk], half_send.at[chunk, 0], half_recv.at[chunk, 0], twin
        )
        first.start()
        solve(chunk, core, mine)
        second = remote(
            mine.at[chunk], other_theirs.at[chunk], half_send.at[chunk, 1], half_recv.at[chunk, 1], twin
        )
        halves += [first, second]
        first.wait_recv()
        for at in range(span):
            f = chunk * span + at

            def pack(k, _):
                held = [ref[chunk, slot, at, k] for ref in (mine, other) for slot in range(2)]
                for (side, r), index in chosen.items():
                    leaving[f, side, r, k] = pick(index, held)
                return 0

            lax.fori_loop(0, levels, pack, 0)
            for r in range(rounds):
                for side, (_, who) in enumerate(ways):
                    sent[f, side, r] = remote(
                        leaving.at[f, side, r],
                        arrived.at[f, side, r],
                        tile_send.at[f, side, r],
                        tile_recv.at[f, side, r],
                        who,
                    )
                    sent[f, side, r].start()
        second.start()

    keys = [(side, r) for side in range(2) for r in range(rounds)]
    passed = {}
    stores = []
    for chunk in range(CHUNKS):
        halves[2 * chunk + 1].wait_recv()

    def place(f):
        chunk, at = f // span, f % span
        for key in keys:
            passed[(f,) + key].wait_recv()

        def level(k, _):
            for part in range(2):
                held, far, came = (
                    (mine, other, arrived) if part == 0 else (theirs, other_theirs, swapped)
                )
                values = [ref[chunk, slot, at, k] for ref in (held, far) for slot in range(2)]
                values += [came[f, side, r, k] for side, r in keys]
                half = core if part == 0 else 1 - core
                for slot in range(2):
                    row = pl.multiple_of(2 * quarter * slot + half * quarter, quarter)
                    result[f, k, pl.ds(row, quarter), :] = pick(origin[slot], values)
            return 0

        lax.fori_loop(0, levels, level, 0)
        store = pltpu.make_async_copy(result.at[f], out_ref.at[f], store_sem.at[f])
        store.start()
        stores.append(store)

    for f in range(fields):
        for side, r in keys:
            sent[f, side, r].wait_recv()
            passed[f, side, r] = remote(
                arrived.at[f, side, r],
                swapped.at[f, side, r],
                swap_send.at[f, side, r],
                swap_recv.at[f, side, r],
                twin,
            )
            passed[f, side, r].start()
        if f > 0:
            place(f - 1)
    place(fields - 1)
    for copy in halves + list(sent.values()) + list(passed.values()):
        copy.wait_send()
    for store in stores:
        store.wait()


def move(rounds, plan, state, diffusivity, mask, north, south, west, east):
    fields, levels, rows, lanes = state.shape
    quarter = rows // 4
    span = fields // CHUNKS
    anywhere = pl.BlockSpec(memory_space=pl.ANY)
    near = pl.BlockSpec(memory_space=pltpu.VMEM)
    halves = pltpu.VMEM((CHUNKS, 2, span, levels, quarter, lanes), F32)
    pieces = pltpu.VMEM((fields, 2, rounds, levels, quarter, lanes), F32)
    dma = pltpu.SemaphoreType.DMA
    return pl.pallas_call(
        functools.partial(move_kernel, rounds),
        in_specs=[pl.BlockSpec(memory_space=pltpu.SMEM), anywhere] + [near] * 6,
        out_specs=anywhere,
        out_shape=jax.ShapeDtypeStruct(state.shape, F32),
        scratch_shapes=[
            pltpu.VMEM((fields, levels, rows + 16, lanes), F32),
            halves,
            halves,
            halves,
            halves,
            pieces,
            pieces,
            pieces,
            pltpu.VMEM(state.shape, F32),
            dma((fields,)),
            dma((fields,)),
            dma((CHUNKS, 2)),
            dma((CHUNKS, 2)),
            dma((fields, 2, rounds)),
            dma((fields, 2, rounds)),
            dma((fields, 2, rounds)),
            dma((fields, 2, rounds)),
        ],
        compiler_params=pltpu.CompilerParams(
            collective_id=rounds, has_side_effects=True, vmem_limit_bytes=(26 + 6 * rounds) * MIB
        ),
    )(plan, state, diffusivity, mask, north, south, west, east)


def local(state, diffusivity, mask, tile_plan):
    plan = tile_plan.reshape(-1)
    north, south, west, east, most = halos(plan, state, mask)
    branches = [functools.partial(move, rounds) for rounds in (1, 2, 3)]
    return lax.switch(most[0], branches, plan, state, diffusivity, mask, north, south, west, east)


def solution(mesh):
    placed = (P(None, None, "lon", "lat"), P(None, "lon", "lat"), P("lon", "lat"), P(None, "lat"))
    return jax.shard_map(
        local, mesh=mesh, in_specs=placed, out_specs=P(None, None, "lon", "lat"), check_vma=False
    )
```

```python
import functools

import jax
import jax.numpy as jnp
from jax import lax
from jax.experimental import pallas as pl
from jax.experimental.pallas import tpu as pltpu
from jax.sharding import PartitionSpec as P

advect_coef = 0.1
diffuse_coef = 0.1
gradient_coef = 0.1
thermal_coef = 0.2
haline_coef = 0.15
weight_coef = 0.25

F32 = jnp.float32
MIB = 1 << 20
MESH = pl.DeviceIdType.MESH
CHUNKS = 4


def halo_kernel(
    plan_ref,
    state_ref,
    mask_ref,
    north_ref,
    south_ref,
    west_ref,
    east_ref,
    most_ref,
    lat_pack,
    lon_pack,
    north_in,
    south_in,
    west_in,
    east_in,
    count,
    counts_in,
    send_sem,
    recv_sem,
):
    levels, rows, lanes = state_ref.shape[1:]
    half = rows // 2
    field = pl.program_id(0)
    last_field = pl.num_programs(0) - 1
    lane = lax.broadcasted_iota(jnp.int32, (8, lanes), 1)
    devices, bands = lax.axis_size("lon"), lax.axis_size("lat")
    lon, lat = lax.axis_index("lon"), lax.axis_index("lat")
    top = lat == bands - 1
    to_east = {"lon": lax.rem(lon + 1, devices)}
    to_west = {"lon": lax.rem(lon + devices - 1, devices)}
    across = {"lon": devices - 1 - lon}
    others = [{"lat": lax.rem(lat + o, bands)} for o in range(1, bands)]
    barrier = pltpu.get_barrier_semaphore()

    @pl.when(field == 0)
    def _():
        for who in [to_east, to_west, across] + others:
            pl.semaphore_signal(barrier, inc=1, device_id=who, device_id_type=MESH)

        lat_pack[...] = jnp.zeros_like(lat_pack)

    unroll = 8

    def group(g, _):
        for sub in range(unroll):
            part = jnp.zeros((8, lanes), F32)
            for slot in range(2):
                at = pl.ds(pl.multiple_of(slot * half + (g * unroll + sub) * 8, 8), 8)
                wet = mask_ref[at, :].astype(F32)
                for k in range(levels):
                    x = state_ref[0, k, at, :] * wet
                    place = 64 * slot + 2 * k
                    part = jnp.where((lane >> 1) == (place >> 1), pltpu.roll(x, place + 1, 1), part)
            to = pl.ds(pl.multiple_of((g * unroll + sub) * 8, 8), 8)
            lat_pack[to, :] += pltpu.roll(part, field * (2 * levels), 1)
        return 0

    lax.fori_loop(0, half // (8 * unroll), group, 0)
    at_field = pl.ds(pl.multiple_of(field * levels, levels), levels)
    first = mask_ref[0:1, :].astype(F32)
    final = mask_ref[rows - 1 : rows, :].astype(F32)
    lon_pack[0, at_field, :] = jnp.concatenate([state_ref[0, k, 0:1, :] for k in range(levels)], 0) * first
    lon_pack[1, at_field, :] = (
        jnp.concatenate([state_ref[0, k, rows - 1 : rows, :] for k in range(levels)], 0) * final
    )

    @pl.when(field == last_field)
    def _():
        chips = devices // 2
        most = jnp.int32(1)
        for chip in range(chips):
            for way in (1, -1):
                number = jnp.int32(0)
                for t in range(4):
                    number = number + leaves(plan_ref, chips, chip, t, way).astype(jnp.int32)
                most = jnp.maximum(most, number)
        count[...] = jnp.full(count.shape, most, jnp.int32)
        pl.semaphore_wait(barrier, 3 + bands - 1)

        def remote(source, target, at, recv_at, who):
            return pltpu.make_async_remote_copy(
                src_ref=source,
                dst_ref=target,
                send_sem=send_sem.at[at],
                recv_sem=recv_sem.at[recv_at],
                device_id=who,
                device_id_type=MESH,
            )

        up = remote(lat_pack, south_in, 0, 0, {"lat": jnp.minimum(lat + 1, bands - 1)})
        down = remote(lat_pack, north_in, 1, 1, {"lat": jnp.maximum(lat - 1, 0)})
        fold = remote(lat_pack, north_in, 0, 1, across)
        east = remote(lon_pack.at[1], west_in, 2, 2, to_east)
        west = remote(lon_pack.at[0], east_in, 3, 3, to_west)
        tell = [remote(count, counts_in.at[o], 4 + o, 4 + o, who) for o, who in enumerate(others)]
        pl.when(top)(fold.start)
        pl.when(jnp.logical_not(top))(up.start)
        pl.when(lat > 0)(down.start)
        east.start()
        west.start()
        for t in tell:
            t.start()

        pl.when(lat > 0)(up.wait_recv)

        @pl.when(lat > 0)
        def _():
            south_ref[...] = south_in[...]

        @pl.when(lat == 0)
        def _():
            south_ref[...] = jnp.zeros_like(south_ref)

        east.wait_recv()
        west_ref[...] = west_in[...]
        west.wait_recv()
        east_ref[...] = east_in[...]
        down.wait_recv()

        @pl.when(top)
        def _():
            r = lax.broadcasted_iota(jnp.int32, (half, half), 0)
            c = lax.broadcasted_iota(jnp.int32, (half, half), 1)
            turn = jnp.where(r + c == half - 1, 1.0, 0.0).astype(F32)
            mirror = jnp.dot(
                turn, north_in[...], precision=lax.Precision.HIGHEST, preferred_element_type=F32
            )
            place = lax.broadcasted_iota(jnp.int32, (half, lanes), 1)
            mirror = pltpu.roll(mirror, 65, 1)
            north_ref[...] = jnp.where((place & 63) >= 32, -mirror, mirror)

        @pl.when(jnp.logical_not(top))
        def _():
            north_ref[...] = north_in[...]

        value = count[...]
        for o, t in enumerate(tell):
            t.wait_recv()
            value = jnp.maximum(value, counts_in[o])
        most_ref[0] = jnp.max(value) - 1
        up.wait_send()
        pl.when(lat > 0)(down.wait_send)
        east.wait_send()
        west.wait_send()
        for t in tell:
            t.wait_send()


def halos(plan, state, mask):
    fields, levels, rows, lanes = state.shape
    bands = lax.axis_size("lat")
    pack = (rows // 2, lanes)
    edge = (fields * levels, lanes)
    spec = lambda shape: pl.BlockSpec(shape, lambda f: (0, 0))
    return pl.pallas_call(
        halo_kernel,
        grid=(fields,),
        in_specs=[
            pl.BlockSpec(memory_space=pltpu.SMEM),
            pl.BlockSpec((1, levels, rows, lanes), lambda f: (f, 0, 0, 0)),
            spec((rows, lanes)),
        ],
        out_specs=[spec(pack), spec(pack), spec(edge), spec(edge), pl.BlockSpec(memory_space=pltpu.SMEM)],
        out_shape=[
            jax.ShapeDtypeStruct(pack, F32),
            jax.ShapeDtypeStruct(pack, F32),
            jax.ShapeDtypeStruct(edge, F32),
            jax.ShapeDtypeStruct(edge, F32),
            jax.ShapeDtypeStruct((1,), jnp.int32),
        ],
        scratch_shapes=[
            pltpu.VMEM(pack, F32),
            pltpu.VMEM((2,) + edge, F32),
            pltpu.VMEM(pack, F32),
            pltpu.VMEM(pack, F32),
            pltpu.VMEM(edge, F32),
            pltpu.VMEM(edge, F32),
            pltpu.VMEM((8, lanes), jnp.int32),
            pltpu.VMEM((bands - 1, 8, lanes), jnp.int32),
            pltpu.SemaphoreType.DMA((4 + bands - 1,)),
            pltpu.SemaphoreType.DMA((4 + bands - 1,)),
        ],
        compiler_params=pltpu.CompilerParams(
            collective_id=0, has_side_effects=True, vmem_limit_bytes=24 * MIB
        ),
    )(plan, state, mask)


def leaves(plan_ref, chips, chip, t, way):
    target = plan_ref[4 * chip + t] // 4
    return target == lax.rem(chip + way + chips, chips)


def pick(index, values):
    chosen = values[0]
    for at, value in enumerate(values[1:], 1):
        chosen = jnp.where(index == at, value, chosen)
    return chosen


def move_kernel(
    rounds,
    plan_ref,
    state_ref,
    diff_ref,
    mask_ref,
    north_ref,
    south_ref,
    west_ref,
    east_ref,
    out_ref,
    padded,
    mine,
    theirs,
    other,
    other_theirs,
    leaving,
    arrived,
    swapped,
    result,
    load_sem,
    store_sem,
    half_send,
    half_recv,
    tile_send,
    tile_recv,
    swap_send,
    swap_recv,
):
    fields, levels, rows, lanes = state_ref.shape
    quarter = rows // 4
    span = fields // CHUNKS
    devices = lax.axis_size("lon")
    chips = devices // 2
    tiles = 4 * chips
    lon = lax.axis_index("lon")
    chip, core = lon // 2, lax.rem(lon, 2)
    twin = {"lon": lon + 1 - 2 * core}
    ahead = {"lon": lax.rem(lon + 2, devices)}
    behind = {"lon": lax.rem(lon + devices - 2, devices)}
    ways = ((1, ahead), (-1, behind))

    barrier = pltpu.get_barrier_semaphore()
    for who in (twin, ahead, behind):
        pl.semaphore_signal(barrier, inc=1, device_id=who, device_id_type=MESH)

    loads = [
        pltpu.make_async_copy(state_ref.at[f], padded.at[f, :, pl.ds(8, rows), :], load_sem.at[f])
        for f in range(fields)
    ]
    for f in (0, 2, 3, 1):
        loads[f].start()

    chosen = {}
    for side, (way, _) in enumerate(ways):
        hits = [leaves(plan_ref, chips, chip, t, way) for t in range(4)]
        for r in range(rounds):
            count, tile = jnp.int32(0), jnp.int32(0)
            for t in range(4):
                tile = jnp.where(hits[t] & (count == r), t, tile)
                count = count + hits[t].astype(jnp.int32)
            chosen[side, r] = jnp.where(tile // 2 == core, 0, 2) + lax.rem(tile, 2)
    origin = []
    for slot in range(2):
        target = 2 * lon + slot
        source = jnp.int32(0)
        for shift in range(-3, 4):
            g = lax.rem(target + shift + tiles, tiles)
            source = jnp.where(plan_ref[g] == target, g, source)
        from_chip, t = source // 4, lax.rem(source, 4)
        at = jnp.where(t // 2 == core, 0, 2) + lax.rem(t, 2)
        for side, (way, _) in enumerate(ways):
            came = from_chip == lax.rem(chip - way + chips, chips)
            rank = jnp.int32(0)
            for q in range(3):
                hit = leaves(plan_ref, chips, from_chip, q, way) & (q < t)
                rank = rank + hit.astype(jnp.int32)
            at = jnp.where(came, 4 + side * rounds + jnp.minimum(rank, rounds - 1), at)
        origin.append(at)

    def cover_field(f):
        def cover(g, _):
            for sub in range(2):
                at = pl.ds(pl.multiple_of(g * 16 + sub * 8, 8), 8)
                to = pl.ds(pl.multiple_of(g * 16 + sub * 8 + 8, 8), 8)
                wet = mask_ref[at, :].astype(F32)
                for k in range(levels):
                    padded[f, k, to, :] = padded[f, k, to, :] * wet
            return 0

        lax.fori_loop(0, rows // 16, cover, 0)
        for k in range(levels):
            i = f * levels + k
            padded[f, k, 7:8, :] = west_ref[i : i + 1, :]
            padded[f, k, rows + 8 : rows + 9, :] = east_ref[i : i + 1, :]

    lane = lax.broadcasted_iota(jnp.int32, (8, lanes), 1)
    is_last = lane == lanes - 1
    is_first = lane == 0

    def solve(chunk, half, to_ref):
        work = list(range(chunk * span, chunk * span + span))
        forced = any(f >= 2 for f in work)
        touched = sorted(set(work) | ({0, 1} if forced else set()))

        def group(step, _):
            slot, g = step // (quarter // 8), lax.rem(step, quarter // 8)
            row = pl.multiple_of(half * quarter + g * 8, 8)
            base = pl.multiple_of(slot * (2 * quarter) + row, 8)
            north_pack = pltpu.roll(north_ref[pl.ds(row, 8), :], 64 * slot, 1)
            south_pack = pltpu.roll(south_ref[pl.ds(row, 8), :], 64 * slot, 1)
            wet = mask_ref[pl.ds(base, 8), :].astype(F32)
            zonal = meridional = None
            upper = []
            rhs = []
            for k in range(levels):
                u = padded[2, k, pl.ds(base + 8, 8), :]
                v = padded[3, k, pl.ds(base + 8, 8), :]
                center, grad_x, grad_y, total = {}, {}, {}, {}
                for f in touched:
                    i = f * levels + k
                    center[f] = {2: u, 3: v}.get(f)
                    if f < 2:
                        center[f] = padded[f, k, pl.ds(base + 8, 8), :]
                    e = padded[f, k, pl.ds(base + 9, 8), :]
                    w = padded[f, k, pl.ds(base + 7, 8), :]
                    n = jnp.where(
                        is_last,
                        pltpu.roll(north_pack, (lanes - 1 - (2 * i + 1)) % lanes, 1),
                        pltpu.roll(center[f], lanes - 1, 1),
                    )
                    s = jnp.where(
                        is_first,
                        pltpu.roll(south_pack, (lanes - 2 * i) % lanes, 1),
                        pltpu.roll(center[f], 1, 1),
                    )
                    grad_x[f] = e - w
                    grad_y[f] = n - s
                    if f in work:
                        total[f] = (e + w) + (n + s)
                if forced:
                    dx = haline_coef * grad_x[1] - thermal_coef * grad_x[0]
                    dy = haline_coef * grad_y[1] - thermal_coef * grad_y[0]
                    zonal = dx if k == 0 else zonal + dx
                    meridional = dy if k == 0 else meridional + dy
                lower_k = diff_ref[k - 1, pl.ds(base, 8), :] if k > 0 else None
                upper_k = diff_ref[k, pl.ds(base, 8), :] if k < levels - 1 else None
                pivot = 1.0
                if k > 0:
                    pivot = pivot + lower_k
                if k < levels - 1:
                    pivot = pivot + upper_k
                if k > 0:
                    pivot = pivot - lower_k * upper[k - 1]
                inverse = 1.0 / pivot
                upper.append(upper_k * inverse if k < levels - 1 else None)
                row_rhs = []
                for at, f in enumerate(work):
                    flow = u * grad_x[f] + v * grad_y[f]
                    value = (1.0 - 4.0 * diffuse_coef) * center[f] + (
                        diffuse_coef * total[f] - advect_coef * flow
                    )
                    if f == 2:
                        value = value - (gradient_coef * weight_coef) * zonal
                    if f == 3:
                        value = value - (gradient_coef * weight_coef) * meridional
                    if k > 0:
                        value = value + lower_k * rhs[k - 1][at]
                    row_rhs.append(value * inverse)
                rhs.append(row_rhs)
            to = pl.ds(pl.multiple_of(g * 8, 8), 8)
            for at, f in enumerate(work):
                x = rhs[levels - 1][at]
                to_ref[chunk, slot, at, levels - 1, to, :] = x * wet
                for k in range(levels - 2, -1, -1):
                    x = rhs[k][at] + upper[k] * x
                    to_ref[chunk, slot, at, k, to, :] = x * wet
            return 0

        lax.fori_loop(0, 2 * (quarter // 8), group, 0)

    def remote(source, target, send, recv, who):
        return pltpu.make_async_remote_copy(
            src_ref=source,
            dst_ref=target,
            send_sem=send,
            recv_sem=recv,
            device_id=who,
            device_id_type=MESH,
        )

    halves = []
    sent = {}
    for chunk in range(CHUNKS):
        for f in (0, 2, 3) if chunk == 0 else (1,) if chunk == 1 else ():
            loads[f].wait()
        for f in range(chunk * span, chunk * span + span):
            cover_field(f)
        solve(chunk, 1 - core, theirs)
        if chunk == 0:
            pl.semaphore_wait(barrier, 3)
        first = remote(
            theirs.at[chunk], other.at[chunk], half_send.at[chunk, 0], half_recv.at[chunk, 0], twin
        )
        first.start()
        solve(chunk, core, mine)
        second = remote(
            mine.at[chunk], other_theirs.at[chunk], half_send.at[chunk, 1], half_recv.at[chunk, 1], twin
        )
        halves += [first, second]
        first.wait_recv()
        for at in range(span):
            f = chunk * span + at

            def pack(k, _):
                held = [ref[chunk, slot, at, k] for ref in (mine, other) for slot in range(2)]
                for (side, r), index in chosen.items():
                    leaving[f, side, r, k] = pick(index, held)
                return 0

            lax.fori_loop(0, levels, pack, 0)
            for r in range(rounds):
                for side, (_, who) in enumerate(ways):
                    sent[f, side, r] = remote(
                        leaving.at[f, side, r],
                        arrived.at[f, side, r],
                        tile_send.at[f, side, r],
                        tile_recv.at[f, side, r],
                        who,
                    )
                    sent[f, side, r].start()
        second.start()

    keys = [(side, r) for side in range(2) for r in range(rounds)]
    passed = {}
    stores = []
    for chunk in range(CHUNKS):
        halves[2 * chunk + 1].wait_recv()

    def place(f):
        chunk, at = f // span, f % span
        for key in keys:
            passed[(f,) + key].wait_recv()

        def level(k, _):
            for part in range(2):
                held, far, came = (
                    (mine, other, arrived) if part == 0 else (theirs, other_theirs, swapped)
                )
                values = [ref[chunk, slot, at, k] for ref in (held, far) for slot in range(2)]
                values += [came[f, side, r, k] for side, r in keys]
                half = core if part == 0 else 1 - core
                for slot in range(2):
                    row = pl.multiple_of(2 * quarter * slot + half * quarter, quarter)
                    result[f, k, pl.ds(row, quarter), :] = pick(origin[slot], values)
            return 0

        lax.fori_loop(0, levels, level, 0)
        store = pltpu.make_async_copy(result.at[f], out_ref.at[f], store_sem.at[f])
        store.start()
        stores.append(store)

    for f in range(fields):
        for side, r in keys:
            sent[f, side, r].wait_recv()
            passed[f, side, r] = remote(
                arrived.at[f, side, r],
                swapped.at[f, side, r],
                swap_send.at[f, side, r],
                swap_recv.at[f, side, r],
                twin,
            )
            passed[f, side, r].start()
        if f > 0:
            place(f - 1)
    place(fields - 1)
    for copy in halves + list(sent.values()) + list(passed.values()):
        copy.wait_send()
    for store in stores:
        store.wait()


def move(rounds, plan, state, diffusivity, mask, north, south, west, east):
    fields, levels, rows, lanes = state.shape
    quarter = rows // 4
    span = fields // CHUNKS
    anywhere = pl.BlockSpec(memory_space=pl.ANY)
    near = pl.BlockSpec(memory_space=pltpu.VMEM)
    halves = pltpu.VMEM((CHUNKS, 2, span, levels, quarter, lanes), F32)
    pieces = pltpu.VMEM((fields, 2, rounds, levels, quarter, lanes), F32)
    dma = pltpu.SemaphoreType.DMA
    return pl.pallas_call(
        functools.partial(move_kernel, rounds),
        in_specs=[pl.BlockSpec(memory_space=pltpu.SMEM), anywhere] + [near] * 6,
        out_specs=anywhere,
        out_shape=jax.ShapeDtypeStruct(state.shape, F32),
        scratch_shapes=[
            pltpu.VMEM((fields, levels, rows + 16, lanes), F32),
            halves,
            halves,
            halves,
            halves,
            pieces,
            pieces,
            pieces,
            pltpu.VMEM(state.shape, F32),
            dma((fields,)),
            dma((fields,)),
            dma((CHUNKS, 2)),
            dma((CHUNKS, 2)),
            dma((fields, 2, rounds)),
            dma((fields, 2, rounds)),
            dma((fields, 2, rounds)),
            dma((fields, 2, rounds)),
        ],
        compiler_params=pltpu.CompilerParams(
            collective_id=rounds, has_side_effects=True, vmem_limit_bytes=(26 + 6 * rounds) * MIB
        ),
    )(plan, state, diffusivity, mask, north, south, west, east)


def local(state, diffusivity, mask, tile_plan):
    plan = tile_plan.reshape(-1)
    north, south, west, east, most = halos(plan, state, mask)
    branches = [functools.partial(move, rounds) for rounds in (1, 2, 3)]
    return lax.switch(most[0], branches, plan, state, diffusivity, mask, north, south, west, east)


def solution(mesh):
    placed = (P(None, None, "lon", "lat"), P(None, "lon", "lat"), P("lon", "lat"), P(None, "lat"))
    return jax.shard_map(
        local, mesh=mesh, in_specs=placed, out_specs=P(None, None, "lon", "lat"), check_vma=False
    )
```
